128 devices in a mesh: blk: 64 (over y, z, x_hi, core), rep: 2 (over x_lo).
Axes of the slice: x: 4 (x_hi: 2, x_lo: 2; x = x_hi * 2 + x_lo), y: 4, z: 4, core: 2. Of those that a mesh axis runs over, the one named last changes fastest.
Arguments:
- picture_vectors: float32 [2, 32768, 1152], P('rep', 'blk'), may hold values from -0.2 to 0.2
- caption_vectors: float32 [2, 32768, 1152], P('rep', 'blk'), may hold values from -0.2 to 0.2
- scale_exponent: float32 [], replicated, may hold values from 2 to 2.5
- offset_shift: float32 [], replicated, may hold values from -6 to -4
Outputs:
- picture_deriv: float32 [2, 32768, 1152], P('rep', 'blk')
- caption_deriv: float32 [2, 32768, 1152], P('rep', 'blk')
- objective_value: float32 [], replicated
- scale_exponent_deriv: float32 [], replicated
- offset_shift_deriv: float32 [], replicated
The draws below stay inside these ranges and needn't reach their ends.
All inputs are finite; a program needn't handle non-finite values.
Results may differ from the reference program's by a relative error of at most 0.00019.
Values sent between devices are 32-bit elements; how exact they have to be, the bound alone decides.
A program may use at most 192 MiB of HBM per device.

```python
import jax
import jax.numpy as jnp
from jax import lax

D = 1152
B_DEV = 512
STEPS = 8
ROWS_BLK = 32768
MATCHED_ENTRIES = 65536
N_BLK = 64
N_REP = 2


def block_levels(rng, shape, shards, low, high):
    def one(position, shards_of):
        heights = jax.random.uniform(jax.random.fold_in(jax.random.fold_in(rng, 6), position), (shards_of,), jnp.float32, low / len(shards), high / len(shards))
        return jnp.repeat(jnp.exp(heights), shape[position] // shards_of).reshape((-1,) + (1,) * (len(shape) - position - 1))

    factor_of = one(*shards[0])
    for cut in shards[1:]:
        factor_of = factor_of * one(*cut)
    return factor_of


def centred(key, extent, deviation, limit, cuts=(), kind=jnp.bfloat16):
    loudness = block_levels(key, extent, cuts, -0.22, 0.18) if cuts else 1.0
    drawn = jax.random.normal(key, extent, jnp.float32) * deviation * loudness
    return jnp.minimum(jnp.maximum(drawn, -limit), limit).astype(kind)


def setup_inputs(seed: int = 0) -> dict:
    keys = jax.random.split(jax.random.key(seed), 5)
    picture_vectors = centred(keys[0], (N_REP, ROWS_BLK, D), 0.03, 0.2, ((0, 2), (1, 64)), jnp.float32)
    caption_vectors = centred(keys[1], (N_REP, ROWS_BLK, D), 0.03, 0.2, ((0, 2), (1, 64)), jnp.float32)
    scale_exponent = jnp.clip(jax.random.uniform(keys[2], (), jnp.float32, 2.0, 2.5), 2.0, 2.5)
    offset_shift = jnp.clip(jax.random.uniform(keys[3], (), jnp.float32, -6.0, -4.0), -6.0, -4.0)
    return {"picture_vectors": picture_vectors, "caption_vectors": caption_vectors, "scale_exponent": scale_exponent, "offset_shift": offset_shift}


EPSILON = 1e-06

def unit_rows(vector):
    row_norm = jnp.sqrt(lax.optimization_barrier(jnp.sum(vector * vector, axis=-1, keepdims=True)) + EPSILON)
    return (vector / row_norm, row_norm)

def unit_backward(grad_unit, unit, row_norm):
    return (grad_unit - unit * lax.optimization_barrier(jnp.sum(unit * grad_unit, axis=-1, keepdims=True))) / row_norm

def reference(picture_vectors, caption_vectors, scale_exponent, offset_shift):
    odds_multiplier = jnp.exp(scale_exponent)
    eye_mask = jnp.eye(B_DEV, dtype=jnp.float32)
    label_home = 2.0 * eye_mask - 1.0
    loss_total = jnp.float32(0.0)
    angular_overall_aggregate = jnp.float32(0.0)
    bias_total = jnp.float32(0.0)
    picture_result = []
    caption_result = []
    for replica in range(N_REP):
        picture_unitlength, image_norm = unit_rows(picture_vectors[replica].reshape(N_BLK, B_DEV, D))
        text_unit, text_norm = unit_rows(caption_vectors[replica].reshape(N_BLK, B_DEV, D))
        picture_running_buffer = jnp.zeros_like(picture_unitlength)
        text_acc = jnp.zeros_like(text_unit)
        for cycle_step in range(STEPS):
            arriving_caption_matrix = jnp.roll(text_unit, cycle_step, axis=0)
            angular_closeness = jnp.einsum('bid,bjd->bij', picture_unitlength, arriving_caption_matrix, precision=lax.Precision.HIGHEST)
            match_sign_target = label_home if cycle_step == 0 else -1.0
            oriented_odds = match_sign_target * (odds_multiplier * angular_closeness + offset_shift)
            loss_total = loss_total + jnp.sum(jax.nn.softplus(-oriented_odds))
            steepness_weight = -match_sign_target * jax.nn.sigmoid(-oriented_odds)
            angular_overall_aggregate = angular_overall_aggregate + jnp.sum(steepness_weight * angular_closeness)
            bias_total = bias_total + jnp.sum(steepness_weight)
            picture_running_buffer = picture_running_buffer + odds_multiplier * jnp.einsum('pxt,ptn->pxn', steepness_weight, arriving_caption_matrix, precision=lax.Precision.HIGHEST)
            caption_share = odds_multiplier * jnp.einsum('iku,ike->iue', steepness_weight, picture_unitlength, precision=lax.Precision.HIGHEST)
            text_acc = text_acc + jnp.roll(caption_share, -cycle_step, axis=0)
        picture_result.append(unit_backward(picture_running_buffer, picture_unitlength, image_norm).reshape(ROWS_BLK, D))
        caption_result.append(unit_backward(text_acc, text_unit, text_norm).reshape(ROWS_BLK, D))
    objective_value = loss_total / MATCHED_ENTRIES
    scale_exponent_deriv = odds_multiplier * angular_overall_aggregate / MATCHED_ENTRIES
    offset_shift_deriv = bias_total / MATCHED_ENTRIES
    return (jnp.stack(picture_result), jnp.stack(caption_result), objective_value, scale_exponent_deriv, offset_shift_deriv)
```

```python
import jax
import jax.numpy as jnp
from jax import lax
from jax.experimental import pallas as pl
from jax.experimental.pallas import tpu as pltpu
from jax.sharding import PartitionSpec as P

MESH = pl.DeviceIdType.MESH
F32 = jnp.float32
BF16 = jnp.bfloat16
EPSILON = 1e-06

N = 512
D = 1152
CHUNKS = 4
R = N // CHUNKS
COLS = [(0, 256), (256, 256), (512, 256), (768, 256), (1024, 128)]

ROW_B, ROW_O, ROW_M, ROW_F = 0, 1024, 1536, 2048
ROWS = 2560
M, B1, B2, B3, C = range(5)
R1, R2, R3, R4, R5 = range(5)
NT = (((1,), (1,)), ((), ()))
NN = (((1,), (0,)), ((), ()))
TN = (((0,), (0,)), ((), ()))


def split(x):
    high = x.astype(BF16)
    return high, (x - high.astype(F32)).astype(BF16)


def dot3(ah, al, bh, bl, dims):
    def one(a, b):
        return lax.dot_general(a, b, dims, preferred_element_type=F32)

    return one(ah, bh) + one(ah, bl) + one(al, bh)


def kernel(
    scale_ref, offset_ref, img, txt,
    out_img, out_txt, out_loss, out_scale, out_offset,
    uih, uil, uth, utl, sh, sl, raw, ret, own, norms, acc, sums, sums_in,
    fs, fr, bs, br, ts, tr, ss, sr, ls,
):
    blk = lax.axis_index("blk")
    rep = lax.axis_index("rep")
    k = blk % 2
    h = (blk // 2) % 2
    m = blk // 4

    def at(dm, hh, kk):
        return (((m + dm + 16) % 16) * 4 + hh * 2 + kk, rep)

    mate = at(0, h, 1 - k)
    after, before = at(1, h, k), at(-1, h, k)
    across = at(0, 1 - h, k)
    diagonal = at(0, 1 - h, 1 - k)
    far = at(2 * k - 1, h, 1 - k)
    odd = at(2 * h - 1, 1 - h, k)
    cube = [(blk + (1 - 2 * ((blk // p) % 2)) * p, rep) for p in (1, 2, 4, 8, 16, 32)] + [(blk, 1 - rep)]

    def remote(src, dst, ssem, rsem, dev):
        return pltpu.make_async_remote_copy(
            src_ref=src, dst_ref=dst, send_sem=ssem, recv_sem=rsem, device_id=dev, device_id_type=MESH
        )

    def rows(i):
        return pl.ds(i * R, R)

    load_img = pltpu.make_async_copy(img, own.at[0], ls.at[0])
    load_txt = pltpu.make_async_copy(txt, own.at[1], ls.at[1])
    load_img.start()
    load_txt.start()

    barrier = pltpu.get_barrier_semaphore()
    partners = [mate, after, before, across, diagonal, far, odd] + cube[2:]
    for dev in partners:
        pl.semaphore_signal(barrier, inc=1, device_id=dev, device_id_type=MESH)
    pl.semaphore_wait(barrier, len(partners))

    def f_text(i):
        return remote(txt.at[rows(i)], raw.at[C, rows(i)], fs.at[0, i], fr.at[C, i], after)

    def f_mate(i):
        return remote(img.at[rows(i)], raw.at[M, rows(i)], fs.at[1, i], fr.at[M, i], mate)

    def f_across(i):
        return remote(img.at[rows(i)], raw.at[B1, rows(i)], fs.at[2, i], fr.at[B1, i], across)

    def f_odd(i):
        return remote(img.at[rows(i)], raw.at[B1, rows(i)], fs.at[2, i], fr.at[B1, i], odd)

    def f_far(i):
        return remote(img.at[rows(i)], raw.at[B3, rows(i)], fs.at[3, i], fr.at[B3, i], far)

    def f_relay(i):
        return remote(raw.at[B3, rows(i)], raw.at[B1, rows(i)], fs.at[4, i], fr.at[B1, i], diagonal)

    def f_pass(i):
        return remote(raw.at[B1, rows(i)], raw.at[B2, rows(i)], fs.at[5, i], fr.at[B2, i], mate)

    h0k1 = (h == 0) & (k == 1)
    for i in range(CHUNKS):
        f_text(i).start()
        pl.when(h == 1)(lambda i=i: f_across(i).start())
        pl.when(h0k1)(lambda i=i: f_odd(i).start())
        pl.when(k == 0)(lambda i=i: f_far(i).start())
        f_mate(i).start()

    scale = jnp.exp(jnp.full((8, 128), scale_ref[0], F32))
    scale11 = scale[0:1, 0:1]
    offset = offset_ref[0]
    acc[...] = jnp.zeros_like(acc)

    def unit(x):
        return x * lax.rsqrt(jnp.sum(x * x, axis=-1, keepdims=True) + EPSILON)

    def put_image(slot, i, row):
        high, low = split(unit(raw[slot, rows(i), :]))
        r = pl.ds(pl.multiple_of(row, R), R)
        uih[r, :] = high
        uil[r, :] = low

    def put_text(i):
        high, low = split(unit(raw[C, rows(i), :]))
        r = pl.ds(N + i * R, R)
        uth[r, :] = high
        utl[r, :] = low

    def slopes(row, n, col, width, home=None):
        r = pl.ds(pl.multiple_of(row, 128), n)
        c = pl.ds(col, width)
        cosine = dot3(uih[r, :], uil[r, :], uth[c, :], utl[c, :], NT)
        z = scale11 * cosine + offset
        if home is not None:
            a = lax.broadcasted_iota(jnp.int32, (n, width), 0) + home
            b = lax.broadcasted_iota(jnp.int32, (n, width), 1)
            sign = jnp.where(a == b, -1.0, 1.0).astype(F32)
            z = sign * z
        e = jnp.exp(z)
        slope = e / (1.0 + e)
        soft = jnp.log1p(e)
        if home is not None:
            slope = sign * slope

        def fold(v):
            v = jnp.sum(v.reshape(n // 8, 8, width), axis=0)
            total = v[:, 0:128]
            for j in range(1, width // 128):
                total = total + v[:, j * 128 : (j + 1) * 128]
            return total

        acc[0:8, :] += fold(soft)
        acc[8:16, :] += fold(slope * cosine)
        acc[16:24, :] += fold(slope)
        high, low = split(scale11 * slope)
        sh[r, c] = high
        sl[r, c] = low

    load_img.wait()
    load_txt.wait()

    @pl.loop(0, CHUNKS)
    def _(i):
        r = pl.ds(pl.multiple_of(i * R, R), R)
        for which in range(2):
            x = own[which, r, :]
            inv = lax.rsqrt(jnp.sum(x * x, axis=-1, keepdims=True) + EPSILON)
            norms[which, r, :] = jnp.broadcast_to(inv, (R, 128))
            high, low = split(x * inv)
            if which == 0:
                q = pl.ds(pl.multiple_of(ROW_O + i * R, R), R)
                uih[q, :] = high
                uil[q, :] = low
            else:
                uth[r, :] = high
                utl[r, :] = low

    @pl.loop(0, 2)
    def _(i):
        slopes(ROW_O + i * 256, 256, 0, 512, home=i * 256)

    for i in range(CHUNKS):
        f_mate(i).wait_recv()
        put_image(M, i, ROW_M + i * R)

    def relay(i):
        @pl.when(h0k1)
        def _():
            f_far(i).wait_recv()
            f_relay(i).start()

    relay(0)

    @pl.when(k == 0)
    def _():
        @pl.loop(0, 2)
        def _(i):
            slopes(ROW_M + i * 256, 256, 0, 512)

    relay(1)

    for i in range(CHUNKS):
        if i + 2 < CHUNKS:
            relay(i + 2)
        f_across(i).wait_recv()
        f_pass(i).start()
        put_image(B1, i, ROW_B + i * 256)
        f_text(i).wait_recv()
        put_text(i)
        f_pass(i).wait_recv()
        put_image(B2, i, ROW_B + i * 256 + R)
        if i < 3:
            slopes(ROW_B + i * 256, 256, 0, 512)
        if i == 1:
            @pl.loop(0, 6)
            def _(j):
                slopes(jnp.where(j < 2, j * 256, ROW_O + (j - 2) * 256), 256, 512, 256)
        if i == 2:
            slopes(ROW_B + 512, 256, 512, 256)

    def g_text(q, d):
        c0, cn = COLS[d]
        cut = (pl.ds(q * 256, 256), pl.ds(c0, cn))
        return remote(raw.at[(C, *cut)], ret.at[(R4, *cut)], ts.at[q * 5 + d], tr.at[q * 5 + d], before)

    def g_pass(j):
        return remote(raw.at[B2, rows(j)], ret.at[R2, rows(j)], bs.at[0, j], br.at[R2, j], mate)

    def g_mate(j):
        return remote(raw.at[M, rows(j)], ret.at[R1, rows(j)], bs.at[1, j], br.at[R1, j], mate)

    def g_across(j):
        return remote(raw.at[B1, rows(j)], ret.at[R3, rows(j)], bs.at[2, j], br.at[R3, j], across)

    def g_odd(j):
        return remote(raw.at[B1, rows(j)], ret.at[R3, rows(j)], bs.at[2, j], br.at[R3, j], odd)

    def g_relay(j):
        return remote(raw.at[B1, rows(j)], ret.at[R5, rows(j)], bs.at[2, j], br.at[R5, j], diagonal)

    def g_far3(j):
        return remote(raw.at[B3, rows(j)], ret.at[R3, rows(j)], bs.at[3, j], br.at[R3, j], far)

    def g_far5(j):
        return remote(raw.at[B3, rows(j)], ret.at[R5, rows(j)], bs.at[3, j], br.at[R5, j], far)

    def image_grad(j):
        f_pass(j).wait_send()
        r = pl.ds(ROW_B + j * 256, 256)
        for c0, cn in COLS:
            c = pl.ds(c0, cn)
            v = dot3(sh[r, :], sl[r, :], uth[:, c], utl[:, c], NN)
            raw[B1, rows(j), c] = v[0:R, :]
            raw[B2, rows(j), c] = v[R:, :]
        g_pass(j).start()

    def image_send(j):
        g_pass(j).wait_recv()
        raw[B1, rows(j), :] += ret[R2, rows(j), :]
        pl.when(h == 0)(lambda: g_across(j).start())
        pl.when((h == 1) & (k == 1))(lambda: g_odd(j).start())
        pl.when((h == 1) & (k == 0))(lambda: g_relay(j).start())

    def text_grad(q, d):
        c0, cn = COLS[d]
        c, t, r = pl.ds(c0, cn), pl.ds(N + q * 256, 256), pl.ds(0, ROW_F)
        raw[C, pl.ds(q * 256, 256), c] = dot3(sh[r, t], sl[r, t], uih[r, c], uil[r, c], TN)

        @pl.when(k == 1)
        def _():
            r = pl.ds(ROW_F, N)
            raw[C, pl.ds(q * 256, 256), c] += dot3(sh[r, t], sl[r, t], uih[r, c], uil[r, c], TN)

        g_text(q, d).start()

    def total(step):
        if step > 0:
            s = step - 1
            remote(sums.at[s], sums_in.at[s], ss.at[s], sr.at[s], cube[s]).wait_recv()
            now = sums[s] + sums_in[s]
        else:
            now = acc[...]
        if step < 7:
            sums[step] = now
            remote(sums.at[step], sums_in.at[step], ss.at[step], sr.at[step], cube[step]).start()
        return now

    slopes(ROW_B, 256, 768, 256)
    image_grad(0)

    slopes(ROW_B + 768, 256, 0, 512)
    slopes(ROW_B + 768, 256, 512, 256)
    image_send(0)

    @pl.when(k == 1)
    def _():
        for i in range(CHUNKS):
            @pl.when(h == 1)
            def _():
                f_far(i).wait_recv()

            put_image(B3, i, ROW_F + i * R)

        @pl.loop(0, 2)
        def _(i):
            slopes(ROW_F + i * 256, 256, 512, 512)

    for d in range(5):
        text_grad(0, d)

    @pl.loop(1, 8)
    def _(j):
        slopes(ROW_B + j * 256, 256, 768, 256)

    image_grad(1)
    total(0)
    text_grad(1, 0)
    image_send(1)
    text_grad(1, 1)
    image_grad(2)
    text_grad(1, 2)
    image_send(2)
    total(1)
    text_grad(1, 3)
    image_grad(3)
    text_grad(1, 4)
    image_send(3)
    total(2)

    @pl.when(k == 1)
    def _():
        for i in range(CHUNKS):
            pl.when(h == 0)(lambda i=i: f_relay(i).wait_send())
        for c0, cn in COLS:
            r, c, t = pl.ds(ROW_F, N), pl.ds(c0, cn), pl.ds(N, N)
            raw[B3, :, c] = dot3(sh[r, t], sl[r, t], uth[t, c], utl[t, c], NN)

        @pl.when(h == 1)
        def _():
            for j in range(CHUNKS):
                g_far5(j).start()

    def far_relay(j):
        @pl.when(h0k1)
        def _():
            g_relay(j).wait_recv()
            raw[B3, rows(j), :] += ret[R5, rows(j), :]
            g_far3(j).start()

    far_relay(0)
    for c0, cn in COLS:
        r, c, t = pl.ds(ROW_M, N), pl.ds(c0, cn), pl.ds(N, N)
        raw[M, :, c] = dot3(sh[r, t], sl[r, t], uth[t, c], utl[t, c], NN)

    @pl.when(k == 0)
    def _():
        for c0, cn in COLS:
            r, c, t = pl.ds(ROW_M, N), pl.ds(c0, cn), pl.ds(0, N)
            raw[M, :, c] += dot3(sh[r, t], sl[r, t], uth[t, c], utl[t, c], NN)

    for j in range(CHUNKS):
        g_mate(j).start()
    total(3)
    far_relay(1)

    for c0, cn in COLS:
        r, c = pl.ds(ROW_O, N), pl.ds(c0, cn)
        own[0, :, c] = dot3(sh[r, :], sl[r, :], uth[:, c], utl[:, c], NN)
    total(4)
    far_relay(2)
    for c0, cn in COLS:
        r, c, t = pl.ds(0, ROW_M), pl.ds(c0, cn), pl.ds(0, N)
        own[1, :, c] = dot3(sh[r, t], sl[r, t], uih[r, c], uil[r, c], TN)

    @pl.when(k == 0)
    def _():
        for c0, cn in COLS:
            r, c, t = pl.ds(ROW_M, N), pl.ds(c0, cn), pl.ds(0, N)
            own[1, :, c] += dot3(sh[r, t], sl[r, t], uih[r, c], uil[r, c], TN)

    total(5)
    far_relay(3)
    total(6)
    final = total(7)

    def whole(v):
        return jnp.sum(jnp.sum(v, axis=0, keepdims=True), axis=1, keepdims=True)

    count = 65536.0
    out_loss[...] = whole(final[0:8, :]) / count
    out_scale[...] = scale11 * whole(final[8:16, :]) / count
    out_offset[...] = whole(final[16:24, :]) / count

    def finish(which, r, n, grad):
        q = pl.ds(ROW_O + r, n)
        u = (uih[q, :].astype(F32) + uil[q, :].astype(F32)) if which == 0 else (
            uth[pl.ds(r, n), :].astype(F32) + utl[pl.ds(r, n), :].astype(F32)
        )
        inv = norms[which, pl.ds(r, n), 0:1]
        along = jnp.sum(u * grad, axis=-1, keepdims=True)
        own[which, pl.ds(r, n), :] = (grad - u * along) * inv

    h1k0 = (h == 1) & (k == 0)

    def store(which, r, n, s):
        dst = (out_img, out_txt)[which]
        return pltpu.make_async_copy(own.at[which, pl.ds(r, n)], dst.at[pl.ds(r, n)], ls.at[s])

    for j in range(CHUNKS):
        g_mate(j).wait_recv()
        g_across(j).wait_recv()

        @pl.when(h1k0)
        def _():
            g_far5(j).wait_recv()
            ret[R3, rows(j), :] += ret[R5, rows(j), :]

        finish(0, j * R, R, own[0, rows(j), :] + ret[R1, rows(j), :] + ret[R3, rows(j), :])
        store(0, j * R, R, j).start()
        if j >= 2:
            q = j - 2
            for d in range(5):
                g_text(q, d).wait_recv()
            for i in range(2):
                r = pl.ds(q * 256 + i * R, R)
                finish(1, q * 256 + i * R, R, own[1, r, :] + ret[R4, r, :])
            store(1, q * 256, 256, 4 + q).start()

    for i in range(CHUNKS):
        f_text(i).wait_send()
        f_mate(i).wait_send()
        pl.when((h == 1) | (k == 1))(lambda i=i: f_across(i).wait_send())
        pl.when(k == 0)(lambda i=i: f_far(i).wait_send())
        g_pass(i).wait_send()
        g_mate(i).wait_send()
        g_across(i).wait_send()
        pl.when(k == 1)(lambda i=i: g_far5(i).wait_send())
    for q in range(2):
        for d in range(5):
            g_text(q, d).wait_send()
    for s in range(7):
        remote(sums.at[s], sums_in.at[s], ss.at[s], sr.at[s], cube[s]).wait_send()
    for j in range(CHUNKS):
        store(0, j * R, R, j).wait()
    for q in range(2):
        store(1, q * 256, 256, 4 + q).wait()


def shards(picture_vectors, caption_vectors, scale_exponent, offset_shift):
    dma = pltpu.SemaphoreType.DMA
    any_space = pl.BlockSpec(memory_space=pl.ANY)
    smem = pl.BlockSpec(memory_space=pltpu.SMEM)
    vmem = pl.BlockSpec(memory_space=pltpu.VMEM)
    block = jax.ShapeDtypeStruct((N, D), F32)
    one = jax.ShapeDtypeStruct((1, 1), F32)
    picture, caption, loss, scale_deriv, offset_deriv = pl.pallas_call(
        kernel,
        out_shape=(block, block, one, one, one),
        in_specs=[smem, smem, any_space, any_space],
        out_specs=(any_space, any_space, vmem, vmem, vmem),
        scratch_shapes=[
            pltpu.VMEM((ROWS, D), BF16),
            pltpu.VMEM((ROWS, D), BF16),
            pltpu.VMEM((2 * N, D), BF16),
            pltpu.VMEM((2 * N, D), BF16),
            pltpu.VMEM((ROWS, 2 * N), BF16),
            pltpu.VMEM((ROWS, 2 * N), BF16),
            pltpu.VMEM((5, N, D), F32),
            pltpu.VMEM((5, N, D), F32),
            pltpu.VMEM((2, N, D), F32),
            pltpu.VMEM((2, N, 128), F32),
            pltpu.VMEM((24, 128), F32),
            pltpu.VMEM((7, 24, 128), F32),
            pltpu.VMEM((7, 24, 128), F32),
            dma((6, CHUNKS)),
            dma((5, CHUNKS)),
            dma((4, CHUNKS)),
            dma((5, CHUNKS)),
            dma((10,)),
            dma((10,)),
            dma((7,)),
            dma((7,)),
            dma((6,)),
        ],
        name="contrastive_window",
        compiler_params=pltpu.CompilerParams(
            collective_id=0, has_side_effects=True, vmem_limit_bytes=63 * 2**20
        ),
    )(
        scale_exponent.reshape(1),
        offset_shift.reshape(1),
        picture_vectors[0],
        caption_vectors[0],
    )
    return (
        picture[None],
        caption[None],
        loss.reshape(()),
        scale_deriv.reshape(()),
        offset_deriv.reshape(()),
    )


def solution(mesh):
    placed = (P("rep", "blk", None), P("rep", "blk", None), P(), P())
    return jax.shard_map(
        shards,
        mesh=mesh,
        in_specs=placed,
        out_specs=(P("rep", "blk", None), P("rep", "blk", None), P(), P(), P()),
        check_vma=False,
    )
```

```python
import jax
import jax.numpy as jnp
from jax import lax
from jax.experimental import pallas as pl
from jax.experimental.pallas import tpu as pltpu
from jax.sharding import PartitionSpec as P

MESH = pl.DeviceIdType.MESH
F32 = jnp.float32
BF16 = jnp.bfloat16
EPSILON = 1e-06

N = 512
D = 1152
CHUNKS = 4
R = N // CHUNKS
PIECES = 8
S = N // PIECES

ROW_B, ROW_O, ROW_M, ROW_F = 0, 1024, 1536, 2048
ROWS = 2560
M, B1, B2, B3, C = range(5)
R1, R2, R3, R4, R5 = range(5)
NT = (((1,), (1,)), ((), ()))
NN = (((1,), (0,)), ((), ()))
TN = (((0,), (0,)), ((), ()))


def split(x):
    high = x.astype(BF16)
    return high, (x - high.astype(F32)).astype(BF16)


def dot3(ah, al, bh, bl, dims):
    def one(a, b):
        return lax.dot_general(a, b, dims, preferred_element_type=F32)

    return one(ah, bh) + one(ah, bl) + one(al, bh)


def kernel(
    scale_ref, offset_ref, img, txt,
    out_img, out_txt, out_loss, out_scale, out_offset,
    uih, uil, uth, utl, sh, sl, raw, ret, own, norms, acc, sums, sums_in, group,
    fs, fr, bs, br, ts, tr, ss, sr, gs, gr, ls,
):
    blk = lax.axis_index("blk")
    rep = lax.axis_index("rep")
    k = blk % 2
    h = (blk // 2) % 2
    m = blk // 4

    def at(dm, hh, kk):
        return (((m + dm + 16) % 16) * 4 + hh * 2 + kk, rep)

    mate = at(0, h, 1 - k)
    after, before = at(1, h, k), at(-1, h, k)
    across = at(0, 1 - h, k)
    diagonal = at(0, 1 - h, 1 - k)
    far = at(2 * k - 1, h, 1 - k)
    odd = at(2 * h - 1, 1 - h, k)
    cube = [(blk + (1 - 2 * ((blk // p) % 2)) * p, rep) for p in (1, 16, 32)]
    place = (m % 4) * 4 + h * 2 + rep

    def group_at(o):
        other = (place + o) % 16
        return (m // 4 * 16 + (other // 4) * 4 + ((other // 2) % 2) * 2 + k, other % 2)


    def remote(src, dst, ssem, rsem, dev):
        return pltpu.make_async_remote_copy(
            src_ref=src, dst_ref=dst, send_sem=ssem, recv_sem=rsem, device_id=dev, device_id_type=MESH
        )

    def rows(i):
        return pl.ds(i * R if isinstance(i, int) else pl.multiple_of(i * R, R), R)

    def piece(p):
        return pl.ds(p * S if isinstance(p, int) else pl.multiple_of(p * S, S), S)

    load_img = pltpu.make_async_copy(img, own.at[0], ls.at[0])
    load_txt = pltpu.make_async_copy(txt, own.at[1], ls.at[1])
    load_img.start()
    load_txt.start()

    barrier = pltpu.get_barrier_semaphore()
    partners = [mate, after, before, across, diagonal, far, odd] + cube[1:] + [group_at(o) for o in range(1, 16)]
    for dev in partners:
        pl.semaphore_signal(barrier, inc=1, device_id=dev, device_id_type=MESH)
    pl.semaphore_wait(barrier, len(partners))

    def f_text(i):
        return remote(txt.at[rows(i)], raw.at[C, rows(i)], fs.at[0, i], fr.at[C, i], after)

    def f_mate(i):
        return remote(img.at[rows(i)], raw.at[M, rows(i)], fs.at[1, i], fr.at[M, i], mate)

    def f_across(i):
        return remote(img.at[rows(i)], raw.at[B1, rows(i)], fs.at[2, i], fr.at[B1, i], across)

    def f_odd(i):
        return remote(img.at[rows(i)], raw.at[B1, rows(i)], fs.at[2, i], fr.at[B1, i], odd)

    def f_far(i):
        return remote(img.at[rows(i)], raw.at[B3, rows(i)], fs.at[3, i], fr.at[B3, i], far)

    def f_relay(i):
        return remote(raw.at[B3, rows(i)], raw.at[B1, rows(i)], fs.at[4, i], fr.at[B1, i], diagonal)

    def f_pass(i):
        return remote(raw.at[B1, rows(i)], raw.at[B2, rows(i)], fs.at[5, i], fr.at[B2, i], mate)

    h0k1 = (h == 0) & (k == 1)

    @pl.loop(0, CHUNKS)
    def _(i):
        f_text(i).start()
        pl.when(h == 1)(lambda: f_across(i).start())
        pl.when(h0k1 & (i == 0))(lambda: f_odd(i).start())
        pl.when(k == 0)(lambda: f_far(i).start())
        f_mate(i).start()

    scale = jnp.exp(jnp.full((8, 128), scale_ref[0], F32))
    scale11 = scale[0:1, 0:1]
    offset = offset_ref[0]
    acc[...] = jnp.zeros_like(acc)

    def unit(x):
        return x * lax.rsqrt(jnp.sum(x * x, axis=-1, keepdims=True) + EPSILON)

    def put_image(slot, i, row):
        high, low = split(unit(raw[slot, rows(i), :]))
        r = pl.ds(pl.multiple_of(row, R), R)
        uih[r, :] = high
        uil[r, :] = low

    def put_text(i):
        high, low = split(unit(raw[C, rows(i), :]))
        r = pl.ds(pl.multiple_of(N + i * R, R), R)
        uth[r, :] = high
        utl[r, :] = low

    def slopes(row, n, col, width, home=None):
        r = pl.ds(pl.multiple_of(row, 128), n)
        c = pl.ds(col, width)
        cosine = dot3(uih[r, :], uil[r, :], uth[c, :], utl[c, :], NT)
        z = scale11 * cosine + offset
        if home is not None:
            a = lax.broadcasted_iota(jnp.int32, (n, width), 0) + home
            b = lax.broadcasted_iota(jnp.int32, (n, width), 1)
            sign = jnp.where(a == b, -1.0, 1.0).astype(F32)
            z = sign * z
        e = jnp.exp(z)
        slope = e / (1.0 + e)
        soft = jnp.log1p(e)
        if home is not None:
            slope = sign * slope

        def fold(v):
            v = jnp.sum(v.reshape(n // 8, 8, width), axis=0)
            total = v[:, 0:128]
            for j in range(1, width // 128):
                total = total + v[:, j * 128 : (j + 1) * 128]
            return total

        acc[0:8, :] += fold(soft)
        acc[8:16, :] += fold(slope * cosine)
        acc[16:24, :] += fold(slope)
        high, low = split(scale11 * slope)
        sh[r, c] = high
        sl[r, c] = low

    load_img.wait()
    load_txt.wait()

    @pl.loop(0, CHUNKS)
    def _(i):
        r = pl.ds(pl.multiple_of(i * R, R), R)
        for which in range(2):
            x = own[which, r, :]
            inv = lax.rsqrt(jnp.sum(x * x, axis=-1, keepdims=True) + EPSILON)
            norms[which, r, :] = jnp.broadcast_to(inv, (R, 128))
            high, low = split(x * inv)
            if which == 0:
                q = pl.ds(pl.multiple_of(ROW_O + i * R, R), R)
                uih[q, :] = high
                uil[q, :] = low
            else:
                uth[r, :] = high
                utl[r, :] = low

    @pl.loop(0, 2)
    def _(i):
        slopes(ROW_O + i * 256, 256, 0, 512, home=i * 256)

    @pl.loop(0, CHUNKS)
    def _(i):
        f_mate(i).wait_recv()
        put_image(M, i, ROW_M + i * R)

    def relay(i):
        @pl.when(h0k1)
        def _():
            f_far(i).wait_recv()
            f_relay(i).start()
            pl.when(i + 1 < CHUNKS)(lambda: f_odd(i + 1).start())

    def g_text(q, d, c):
        cut = (pl.ds(q * 256, 256), c)
        return remote(raw.at[(C, *cut)], ret.at[(R4, *cut)], ts.at[q * 5 + d], tr.at[q * 5 + d], before)

    def g_pass(j):
        return remote(raw.at[B2, rows(j)], ret.at[R2, rows(j)], bs.at[0, j], br.at[R2, j], mate)

    def g_mate(j):
        return remote(raw.at[M, rows(j)], ret.at[R1, rows(j)], bs.at[1, j], br.at[R1, j], mate)

    def g_across(p):
        return remote(raw.at[B1, piece(p)], ret.at[R3, piece(p)], bs.at[2, p], br.at[R3, p], across)

    def g_odd(p):
        return remote(raw.at[B1, piece(p)], ret.at[R3, piece(p)], bs.at[2, p], br.at[R3, p], odd)

    def g_relay(p):
        return remote(raw.at[B1, piece(p)], ret.at[R5, piece(p)], bs.at[2, p], br.at[R5, p], diagonal)

    def g_far3(p):
        return remote(raw.at[B3, piece(p)], ret.at[R3, piece(p)], bs.at[3, p], br.at[R3, p], far)

    def g_far5(p):
        return remote(raw.at[B3, piece(p)], ret.at[R5, piece(p)], bs.at[3, p], br.at[R5, p], far)

    def put(dst, value, first):
        if first:
            dst[...] = value
        else:
            dst[...] += value

    def columns(body):
        @pl.loop(0, 4)
        def _(d):
            body(d, pl.ds(pl.multiple_of(d * 256, 256), 256))

        body(4, pl.ds(1024, 128))

    def image_part(dst, row, col, width, first, n=N):
        r, t = pl.ds(row, n), pl.ds(col, width)

        def body(d, c):
            put(dst.at[:, c], dot3(sh[r, t], sl[r, t], uth[t, c], utl[t, c], NN), first)

        columns(body)

    def next_part(j, col, width, first):
        r, t, q = pl.ds(pl.multiple_of(ROW_B + j * 256, 256), 256), pl.ds(col, width), rows(j)

        def body(d, c):
            v = dot3(sh[r, t], sl[r, t], uth[t, c], utl[t, c], NN)
            put(raw.at[B1, q, c], v[0:R, :], first)
            put(raw.at[B2, q, c], v[R:, :], first)

        columns(body)

    def text_part(dst, row, n, col, width, first, then=None):
        r, t = pl.ds(row, n), pl.ds(col, width)

        def body(d, c):
            put(dst.at[:, c], dot3(sh[r, t], sl[r, t], uih[r, c], uil[r, c], TN), first)
            if then is not None:
                then(d, c)

        columns(body)

    first_half, second_half = raw.at[C, pl.ds(0, 256)], raw.at[C, pl.ds(256, 256)]
    HALF0, HALF1 = N, N + 256

    relay(0)

    @pl.when(k == 0)
    def _():
        @pl.loop(0, 2)
        def _(i):
            slopes(ROW_M + i * 256, 256, 0, N)

        image_part(raw.at[M], ROW_M, 0, N, True)

    image_part(own.at[0], ROW_O, 0, N, True)
    relay(1)
    text_part(own.at[1], ROW_O, N, 0, N, True)

    @pl.when(k == 0)
    def _():
        text_part(own.at[1], ROW_M, N, 0, N, False)

    def arrive(i, last=False):
        f_across(i).wait_recv()
        f_pass(i).start()
        put_image(B1, i, ROW_B + i * 256)
        if not last:
            pl.when(i < 2)(lambda: relay(i + 2))
        f_text(i).wait_recv()
        put_text(i)
        f_pass(i).wait_recv()
        put_image(B2, i, ROW_B + i * 256 + R)

    @pl.loop(0, 3)
    def _(i):
        arrive(i)

        @pl.when(i < 2)
        def _():
            slopes(ROW_B + i * 256, 256, 0, 512)
            pl.when(i == 0)(lambda: text_part(own.at[1], ROW_B, 256, 0, N, False))

        @pl.when(i == 1)
        def _():
            @pl.loop(0, 6)
            def _(j):
                slopes(jnp.where(j < 2, j * 256, ROW_O + (j - 2) * 256), 256, HALF0, 256)

            text_part(first_half, ROW_B, 512, HALF0, 256, True)
            text_part(first_half, ROW_O, 1024, HALF0, 256, False)
            f_pass(0).wait_send()
            next_part(0, 0, 768, True)

    slopes(ROW_B + 512, 256, 0, 768)
    text_part(first_half, ROW_B + 512, 256, HALF0, 256, False)

    def next_send(j):
        g_pass(j).wait_recv()
        raw[B1, rows(j), :] += ret[R2, rows(j), :]

        @pl.loop(0, PIECES // CHUNKS)
        def _(e):
            p = j * (PIECES // CHUNKS) + e
            pl.when(h == 0)(lambda: g_across(p).start())
            pl.when((h == 1) & (k == 1))(lambda: g_odd(p).start())
            pl.when((h == 1) & (k == 0))(lambda: g_relay(p).start())

    def total(step):
        if step == 0:
            now = jnp.concatenate(
                [jnp.sum(acc[8 * q : 8 * q + 8, :], axis=0, keepdims=True) for q in range(3)]
                + [jnp.zeros((5, 128), F32)],
                axis=0,
            )
        else:
            s = step - 1
            remote(sums.at[s], sums_in.at[s], ss.at[s], sr.at[s], cube[s]).wait_recv()
            now = sums[s] + sums_in[s]
        if step < 3:
            sums[step] = now
            remote(sums.at[step], sums_in.at[step], ss.at[step], sr.at[step], cube[step]).start()
        else:
            group[place] = now
            for o in range(1, 16):
                share(o).start()

    def share(o):
        return remote(group.at[place], group.at[place], gs.at[o], gr.at[o], group_at(o))

    arrive(3, True)
    slopes(ROW_B, 256, HALF1, 256)
    next_part(0, HALF1, 256, False)
    g_pass(0).start()
    slopes(ROW_B + 256, 256, HALF1, 256)
    next_send(0)
    f_pass(1).wait_send()
    next_part(1, 0, 1024, True)
    g_pass(1).start()
    slopes(ROW_B + 768, 256, 0, 768)
    next_send(1)

    def far_relay(p):
        @pl.when(h0k1)
        def _():
            g_relay(p).wait_recv()
            raw[B3, piece(p), :] += ret[R5, piece(p), :]
            g_far3(p).start()

    @pl.when(k == 1)
    def _():
        @pl.loop(0, CHUNKS)
        def _(i):
            pl.when(h == 1)(lambda: f_far(i).wait_recv())
            put_image(B3, i, ROW_F + i * R)

        @pl.loop(0, 2)
        def _(i):
            slopes(ROW_F + i * 256, 256, N, N)

        text_part(first_half, ROW_F, N, HALF0, 256, False)

    text_part(first_half, ROW_B + 768, 256, HALF0, 256, False, lambda d, c: g_text(0, d, c).start())

    @pl.when(k == 1)
    def _():
        @pl.when(h == 0)
        def _():
            @pl.loop(0, CHUNKS)
            def _(i):
                f_relay(i).wait_send()

        image_part(raw.at[B3], ROW_F, N, N, True)

        @pl.when(h == 1)
        def _():
            @pl.loop(0, PIECES)
            def _(p):
                g_far5(p).start()

    @pl.loop(2, 4)
    def _(j):
        pl.when(j == 2)(lambda: slopes(ROW_B + 512, 256, HALF1, 256))
        f_pass(j).wait_send()
        next_part(j, 0, 1024, True)
        g_pass(j).start()

        @pl.when(j == 2)
        def _():
            @pl.loop(3, 8)
            def _(i):
                slopes(ROW_B + i * 256, 256, HALF1, 256)

            far_relay(0)
            far_relay(1)
            next_send(2)
            total(0)
            text_part(second_half, 0, 1024, HALF1, 256, True)

            @pl.when(k == 1)
            def _():
                text_part(second_half, ROW_F, N, HALF1, 256, False)

            total(1)
            text_part(second_half, ROW_O, 1024, HALF1, 256, False, lambda d, c: g_text(1, d, c).start())
            far_relay(2)
            far_relay(3)

    total(2)
    next_send(3)

    @pl.when(k == 0)
    def _():
        image_part(raw.at[M], ROW_M, N, N, False)

    @pl.when(k == 1)
    def _():
        image_part(raw.at[M], ROW_M, N, N, True)

    @pl.loop(0, CHUNKS)
    def _(j):
        g_mate(j).start()

    far_relay(4)
    total(3)

    image_part(own.at[0], ROW_O, N, N, False)
    far_relay(5)
    text_part(own.at[1], ROW_B + 256, 768, 0, N, False)

    def whole(v):
        return jnp.sum(jnp.sum(v, axis=0, keepdims=True), axis=1, keepdims=True)

    def finish(which, r, n, grad):
        r = pl.multiple_of(r, n)
        high, low, q = (uih, uil, pl.ds(pl.multiple_of(ROW_O + r, n), n)) if which == 0 else (uth, utl, pl.ds(r, n))
        u = high[q, :].astype(F32) + low[q, :].astype(F32)
        inv = norms[which, pl.ds(r, n), 0:1]
        along = jnp.sum(u * grad, axis=-1, keepdims=True)
        own[which, pl.ds(r, n), :] = (grad - u * along) * inv

    h1k0 = (h == 1) & (k == 0)

    def store(which, r, n, s):
        dst = (out_img, out_txt)[which]
        r = pl.multiple_of(r, n)
        return pltpu.make_async_copy(own.at[which, pl.ds(r, n)], dst.at[pl.ds(r, n)], ls.at[s])

    @pl.loop(0, PIECES)
    def _(p):
        pl.when(p < 2)(lambda: far_relay(p + 6))
        pl.when(p % 2 == 0)(lambda: g_mate(p // 2).wait_recv())
        g_across(p).wait_recv()

        @pl.when(h1k0)
        def _():
            g_far5(p).wait_recv()
            ret[R3, piece(p), :] += ret[R5, piece(p), :]

        finish(0, p * S, S, own[0, piece(p), :] + ret[R1, piece(p), :] + ret[R3, piece(p), :])
        store(0, p * S, S, p).start()

        @pl.when(p % 4 == 2)
        def _():
            q = p // 4
            columns(lambda d, c: g_text(q, d, c).wait_recv())

            @pl.loop(0, 2)
            def _(i):
                start = pl.multiple_of(q * 256 + i * R, R)
                r = pl.ds(start, R)
                finish(1, start, R, own[1, r, :] + ret[R4, r, :])

            store(1, pl.multiple_of(q * 256, 256), 256, PIECES + q).start()

    for o in range(1, 16):
        share(o).wait_recv()
    final = group[0]
    for o in range(1, 16):
        final = final + group[o]

    count = 65536.0
    out_loss[...] = whole(final[0:1, :]) / count
    out_scale[...] = scale11 * whole(final[1:2, :]) / count
    out_offset[...] = whole(final[2:3, :]) / count

    @pl.loop(0, CHUNKS)
    def _(i):
        f_text(i).wait_send()
        f_mate(i).wait_send()
        pl.when((h == 1) | (k == 1))(lambda: f_across(i).wait_send())
        pl.when(k == 0)(lambda: f_far(i).wait_send())
        g_pass(i).wait_send()
        g_mate(i).wait_send()

    @pl.loop(0, PIECES)
    def _(p):
        g_across(p).wait_send()
        pl.when(k == 1)(lambda: g_far5(p).wait_send())
        store(0, p * S, S, p).wait()

    for q in range(2):
        columns(lambda d, c, q=q: g_text(q, d, c).wait_send())
        store(1, q * 256, 256, PIECES + q).wait()
    for s in range(3):
        remote(sums.at[s], sums_in.at[s], ss.at[s], sr.at[s], cube[s]).wait_send()
    for o in range(1, 16):
        share(o).wait_send()


def shards(picture_vectors, caption_vectors, scale_exponent, offset_shift):
    dma = pltpu.SemaphoreType.DMA
    any_space = pl.BlockSpec(memory_space=pl.ANY)
    smem = pl.BlockSpec(memory_space=pltpu.SMEM)
    vmem = pl.BlockSpec(memory_space=pltpu.VMEM)
    block = jax.ShapeDtypeStruct((N, D), F32)
    one = jax.ShapeDtypeStruct((1, 1), F32)
    picture, caption, loss, scale_deriv, offset_deriv = pl.pallas_call(
        kernel,
        out_shape=(block, block, one, one, one),
        in_specs=[smem, smem, any_space, any_space],
        out_specs=(any_space, any_space, vmem, vmem, vmem),
        scratch_shapes=[
            pltpu.VMEM((ROWS, D), BF16),
            pltpu.VMEM((ROWS, D), BF16),
            pltpu.VMEM((2 * N, D), BF16),
            pltpu.VMEM((2 * N, D), BF16),
            pltpu.VMEM((ROWS, 2 * N), BF16),
            pltpu.VMEM((ROWS, 2 * N), BF16),
            pltpu.VMEM((5, N, D), F32),
            pltpu.VMEM((5, N, D), F32),
            pltpu.VMEM((2, N, D), F32),
            pltpu.VMEM((2, N, 128), F32),
            pltpu.VMEM((24, 128), F32),
            pltpu.VMEM((3, 8, 128), F32),
            pltpu.VMEM((3, 8, 128), F32),
            pltpu.VMEM((16, 8, 128), F32),
            dma((6, CHUNKS)),
            dma((5, CHUNKS)),
            dma((4, PIECES)),
            dma((5, PIECES)),
            dma((10,)),
            dma((10,)),
            dma((3,)),
            dma((3,)),
            dma((16,)),
            dma((16,)),
            dma((PIECES + 2,)),
        ],
        name="contrastive_window",
        compiler_params=pltpu.CompilerParams(
            collective_id=0, has_side_effects=True, vmem_limit_bytes=63 * 2**20
        ),
    )(
        scale_exponent.reshape(1),
        offset_shift.reshape(1),
        picture_vectors[0],
        caption_vectors[0],
    )
    return (
        picture[None],
        caption[None],
        loss.reshape(()),
        scale_deriv.reshape(()),
        offset_deriv.reshape(()),
    )


def solution(mesh):
    placed = (P("rep", "blk", None), P("rep", "blk", None), P(), P())
    return jax.shard_map(
        shards,
        mesh=mesh,
        in_specs=placed,
        out_specs=(P("rep", "blk", None), P("rep", "blk", None), P(), P(), P()),
        check_vma=False,
    )
```

```python
import jax
import jax.numpy as jnp
from jax import lax
from jax.experimental import pallas as pl
from jax.experimental.pallas import tpu as pltpu
from jax.sharding import PartitionSpec as P

MESH = pl.DeviceIdType.MESH
F32 = jnp.float32
BF16 = jnp.bfloat16
EPSILON = 1e-06

N = 512
D = 1152
CHUNKS = 4
R = N // CHUNKS
PIECES = 8
S = N // PIECES

ROW_B, ROW_O, ROW_M, ROW_F = 0, 1024, 1536, 2048
ROWS = 2560
M, B1, B2, B3, C = range(5)
R1, R2, R3, R4, R5 = range(5)
NT = (((1,), (1,)), ((), ()))
NN = (((1,), (0,)), ((), ()))
TN = (((0,), (0,)), ((), ()))


def split(x):
    high = x.astype(BF16)
    return high, (x - high.astype(F32)).astype(BF16)


def dot3(ah, al, bh, bl, dims):
    def one(a, b):
        return lax.dot_general(a, b, dims, preferred_element_type=F32)

    return one(ah, bh) + one(ah, bl) + one(al, bh)


def kernel(
    scale_ref, offset_ref, img, txt,
    out_img, out_txt, out_loss, out_scale, out_offset,
    uih, uil, uth, utl, sh, sl, raw, ret, own, norms, acc, column, group, given, sums,
    fs, fr, bs, br, ts, tr, cs, cr, gs, gr, ls, vs,
):
    blk = lax.axis_index("blk")
    rep = lax.axis_index("rep")
    k = blk % 2
    h = (blk // 2) % 2
    m = blk // 4

    def at(dm, hh, kk):
        return (((m + dm + 16) % 16) * 4 + hh * 2 + kk, rep)

    mate = at(0, h, 1 - k)
    after, before = at(1, h, k), at(-1, h, k)
    across = at(0, 1 - h, k)
    diagonal = at(0, 1 - h, 1 - k)
    far = at(2 * k - 1, h, 1 - k)
    odd = at(2 * h - 1, 1 - h, k)
    level = (m // 4) * 2 + k

    def column_at(o):
        other = (level + o) % 8
        return ((other // 2) * 16 + (m % 4) * 4 + h * 2 + other % 2, rep)

    place = (m % 4) * 4 + h * 2 + rep

    def group_at(o):
        other = (place + o) % 16
        return (m // 4 * 16 + (other // 4) * 4 + ((other // 2) % 2) * 2 + k, other % 2)


    def remote(src, dst, ssem, rsem, dev):
        return pltpu.make_async_remote_copy(
            src_ref=src, dst_ref=dst, send_sem=ssem, recv_sem=rsem, device_id=dev, device_id_type=MESH
        )

    def rows(i):
        return pl.ds(i * R if isinstance(i, int) else pl.multiple_of(i * R, R), R)

    def piece(p):
        return pl.ds(p * S if isinstance(p, int) else pl.multiple_of(p * S, S), S)

    load_img = pltpu.make_async_copy(img, own.at[0], ls.at[0])
    load_txt = pltpu.make_async_copy(txt, own.at[1], ls.at[1])
    load_img.start()
    load_txt.start()
    load_scale = pltpu.make_async_copy(scale_ref, given.at[0], vs.at[0])
    load_offset = pltpu.make_async_copy(offset_ref, given.at[1], vs.at[1])
    load_scale.start()
    load_offset.start()

    barrier = pltpu.get_barrier_semaphore()
    partners = [mate, after, before, across, diagonal, far, odd]
    partners += [column_at(o) for o in range(1, 8)] + [group_at(o) for o in range(1, 16)]
    for dev in partners:
        pl.semaphore_signal(barrier, inc=1, device_id=dev, device_id_type=MESH)
    pl.semaphore_wait(barrier, len(partners))

    def f_text(i):
        return remote(txt.at[rows(i)], raw.at[C, rows(i)], fs.at[0, i], fr.at[C, i], after)

    def f_mate(i):
        return remote(img.at[rows(i)], raw.at[M, rows(i)], fs.at[1, i], fr.at[M, i], mate)

    def f_across(i):
        return remote(img.at[rows(i)], raw.at[B1, rows(i)], fs.at[2, i], fr.at[B1, i], across)

    def f_odd(i):
        return remote(img.at[rows(i)], raw.at[B1, rows(i)], fs.at[2, i], fr.at[B1, i], odd)

    def f_far(i):
        return remote(img.at[rows(i)], raw.at[B3, rows(i)], fs.at[3, i], fr.at[B3, i], far)

    def f_relay(i):
        return remote(raw.at[B3, rows(i)], raw.at[B1, rows(i)], fs.at[4, i], fr.at[B1, i], diagonal)

    def f_pass(i):
        return remote(raw.at[B1, rows(i)], raw.at[B2, rows(i)], fs.at[5, i], fr.at[B2, i], mate)

    h0k1 = (h == 0) & (k == 1)

    @pl.loop(0, CHUNKS)
    def _(i):
        f_text(i).start()
        pl.when(h == 1)(lambda: f_across(i).start())
        pl.when(h0k1 & (i == 0))(lambda: f_odd(i).start())
        pl.when(k == 0)(lambda: f_far(i).start())
        f_mate(i).start()

    load_scale.wait()
    load_offset.wait()
    scale11 = jnp.exp(given[0])
    offset = given[1]
    acc[...] = jnp.zeros_like(acc)

    def unit(x):
        return x * lax.rsqrt(jnp.sum(x * x, axis=-1, keepdims=True) + EPSILON)

    def put_image(slot, i, row):
        high, low = split(unit(raw[slot, rows(i), :]))
        r = pl.ds(pl.multiple_of(row, R), R)
        uih[r, :] = high
        uil[r, :] = low

    def put_text(i):
        high, low = split(unit(raw[C, rows(i), :]))
        r = pl.ds(pl.multiple_of(N + i * R, R), R)
        uth[r, :] = high
        utl[r, :] = low

    def slopes(row, n, col, width, home=None):
        r = pl.ds(pl.multiple_of(row, 128), n)
        c = pl.ds(col, width)
        cosine = dot3(uih[r, :], uil[r, :], uth[c, :], utl[c, :], NT)
        z = scale11 * cosine + offset
        if home is not None:
            a = lax.broadcasted_iota(jnp.int32, (n, width), 0) + home
            b = lax.broadcasted_iota(jnp.int32, (n, width), 1)
            sign = jnp.where(a == b, -1.0, 1.0).astype(F32)
            z = sign * z
        e = jnp.exp(z)
        slope = e / (1.0 + e)
        soft = jnp.log1p(e)
        if home is not None:
            slope = sign * slope

        def fold(v):
            v = jnp.sum(v.reshape(n // 8, 8, width), axis=0)
            total = v[:, 0:128]
            for j in range(1, width // 128):
                total = total + v[:, j * 128 : (j + 1) * 128]
            return total

        acc[0:8, :] += fold(soft)
        acc[8:16, :] += fold(slope * cosine)
        acc[16:24, :] += fold(slope)
        high, low = split(scale11 * slope)
        sh[r, c] = high
        sl[r, c] = low

    load_img.wait()
    load_txt.wait()

    @pl.loop(0, CHUNKS)
    def _(i):
        r = pl.ds(pl.multiple_of(i * R, R), R)
        for which in range(2):
            x = own[which, r, :]
            inv = lax.rsqrt(jnp.sum(x * x, axis=-1, keepdims=True) + EPSILON)
            norms[which, r, :] = jnp.broadcast_to(inv, (R, 128))
            high, low = split(x * inv)
            if which == 0:
                q = pl.ds(pl.multiple_of(ROW_O + i * R, R), R)
                uih[q, :] = high
                uil[q, :] = low
            else:
                uth[r, :] = high
                utl[r, :] = low

    @pl.loop(0, 2)
    def _(i):
        slopes(ROW_O + i * 256, 256, 0, 512, home=i * 256)

    @pl.loop(0, CHUNKS)
    def _(i):
        f_mate(i).wait_recv()
        put_image(M, i, ROW_M + i * R)

    def relay(i):
        @pl.when(h0k1)
        def _():
            f_far(i).wait_recv()
            f_relay(i).start()
            pl.when(i + 1 < CHUNKS)(lambda: f_odd(i + 1).start())

    def g_text(q, d, c):
        cut = (pl.ds(q * 256, 256), c)
        return remote(raw.at[(C, *cut)], ret.at[(R4, *cut)], ts.at[q * 5 + d], tr.at[q * 5 + d], before)

    def g_pass(j):
        return remote(raw.at[B2, rows(j)], ret.at[R2, rows(j)], bs.at[0, j], br.at[R2, j], mate)

    def g_mate(j):
        return remote(raw.at[M, rows(j)], ret.at[R1, rows(j)], bs.at[1, j], br.at[R1, j], mate)

    def g_across(p):
        return remote(raw.at[B1, piece(p)], ret.at[R3, piece(p)], bs.at[2, p], br.at[R3, p], across)

    def g_odd(p):
        return remote(raw.at[B1, piece(p)], ret.at[R3, piece(p)], bs.at[2, p], br.at[R3, p], odd)

    def g_relay(p):
        return remote(raw.at[B1, piece(p)], ret.at[R5, piece(p)], bs.at[2, p], br.at[R5, p], diagonal)

    def g_far3(p):
        return remote(raw.at[B3, piece(p)], ret.at[R3, piece(p)], bs.at[3, p], br.at[R3, p], far)

    def g_far5(p):
        return remote(raw.at[B3, piece(p)], ret.at[R5, piece(p)], bs.at[3, p], br.at[R5, p], far)

    def put(dst, value, first):
        if first:
            dst[...] = value
        else:
            dst[...] += value

    def columns(body):
        @pl.loop(0, 4)
        def _(d):
            body(d, pl.ds(pl.multiple_of(d * 256, 256), 256))

        body(4, pl.ds(1024, 128))

    def image_part(dst, row, col, width, first, n=N):
        r, t = pl.ds(row, n), pl.ds(col, width)

        def body(d, c):
            put(dst.at[:, c], dot3(sh[r, t], sl[r, t], uth[t, c], utl[t, c], NN), first)

        columns(body)

    def next_part(j, col, width, first):
        r, t, q = pl.ds(pl.multiple_of(ROW_B + j * 256, 256), 256), pl.ds(col, width), rows(j)

        def body(d, c):
            v = dot3(sh[r, t], sl[r, t], uth[t, c], utl[t, c], NN)
            put(raw.at[B1, q, c], v[0:R, :], first)
            put(raw.at[B2, q, c], v[R:, :], first)

        columns(body)

    def text_part(dst, row, n, col, width, first, then=None):
        r, t = pl.ds(row, n), pl.ds(col, width)

        def body(d, c):
            put(dst.at[:, c], dot3(sh[r, t], sl[r, t], uih[r, c], uil[r, c], TN), first)
            if then is not None:
                then(d, c)

        columns(body)

    first_half, second_half = raw.at[C, pl.ds(0, 256)], raw.at[C, pl.ds(256, 256)]
    HALF0, HALF1 = N, N + 256

    relay(0)

    @pl.when(k == 0)
    def _():
        @pl.loop(0, 2)
        def _(i):
            slopes(ROW_M + i * 256, 256, 0, N)

        image_part(raw.at[M], ROW_M, 0, N, True)

    image_part(own.at[0], ROW_O, 0, N, True)
    relay(1)
    text_part(own.at[1], ROW_O, N, 0, N, True)

    @pl.when(k == 0)
    def _():
        text_part(own.at[1], ROW_M, N, 0, N, False)

    def arrive(i):
        f_across(i).wait_recv()
        f_pass(i).start()
        put_image(B1, i, ROW_B + i * 256)
        pl.when(i < 2)(lambda: relay(i + 2))
        f_text(i).wait_recv()
        put_text(i)
        f_pass(i).wait_recv()
        put_image(B2, i, ROW_B + i * 256 + R)

    @pl.loop(0, 3)
    def _(i):
        arrive(i)

        @pl.when(i < 2)
        def _():
            slopes(ROW_B + i * 256, 256, 0, 512)
            pl.when(i == 0)(lambda: text_part(own.at[1], ROW_B, 256, 0, N, False))

        @pl.when(i == 1)
        def _():
            @pl.loop(0, 6)
            def _(j):
                slopes(jnp.where(j < 2, j * 256, ROW_O + (j - 2) * 256), 256, HALF0, 256)

            text_part(first_half, ROW_B, 512, HALF0, 256, True)
            text_part(first_half, ROW_O, 1024, HALF0, 256, False)
            f_pass(0).wait_send()
            next_part(0, 0, 768, True)

    slopes(ROW_B + 512, 256, 0, 768)
    text_part(first_half, ROW_B + 512, 256, HALF0, 256, False)

    def next_send(j):
        g_pass(j).wait_recv()
        raw[B1, rows(j), :] += ret[R2, rows(j), :]

        @pl.loop(0, PIECES // CHUNKS)
        def _(e):
            p = j * (PIECES // CHUNKS) + e
            pl.when(h == 0)(lambda: g_across(p).start())
            pl.when((h == 1) & (k == 0))(lambda: g_relay(p).start())

    def odd_send(j):
        @pl.when((h == 1) & (k == 1))
        def _():
            @pl.loop(0, PIECES // CHUNKS)
            def _(e):
                g_odd(j * (PIECES // CHUNKS) + e).start()

    def column_share(o):
        return remote(column.at[level], column.at[level], cs.at[o], cr.at[o], column_at(o))

    def share(o):
        return remote(group.at[place], group.at[place], gs.at[o], gr.at[o], group_at(o))

    def share_column():
        column[level] = jnp.concatenate(
            [jnp.sum(acc[8 * q : 8 * q + 8, :], axis=0, keepdims=True) for q in range(3)]
            + [jnp.zeros((5, 128), F32)],
            axis=0,
        )
        for o in range(1, 8):
            column_share(o).start()

    def share_group():
        for o in range(1, 8):
            column_share(o).wait_recv()
        now = column[0]
        for o in range(1, 8):
            now = now + column[o]
        group[place] = now
        for o in range(1, 16):
            share(o).start()

    f_text(3).wait_recv()
    put_text(3)
    slopes(ROW_B, 256, HALF1, 256)
    next_part(0, HALF1, 256, False)
    g_pass(0).start()
    f_across(3).wait_recv()
    f_pass(3).start()
    put_image(B1, 3, ROW_B + 768)
    slopes(ROW_B + 256, 256, HALF1, 256)
    next_send(0)
    odd_send(0)
    f_pass(3).wait_recv()
    put_image(B2, 3, ROW_B + 768 + R)
    f_pass(1).wait_send()
    next_part(1, 0, 1024, True)
    g_pass(1).start()
    slopes(ROW_B + 768, 256, 0, 768)
    next_send(1)
    odd_send(1)

    def far_relay(p):
        @pl.when(h0k1)
        def _():
            g_relay(p).wait_recv()
            raw[B3, piece(p), :] += ret[R5, piece(p), :]
            g_far3(p).start()

    @pl.when(k == 1)
    def _():
        @pl.loop(0, CHUNKS)
        def _(i):
            pl.when(h == 1)(lambda: f_far(i).wait_recv())
            put_image(B3, i, ROW_F + i * R)

        @pl.loop(0, 2)
        def _(i):
            slopes(ROW_F + i * 256, 256, N, N)

        text_part(first_half, ROW_F, N, HALF0, 256, False)

    text_part(first_half, ROW_B + 768, 256, HALF0, 256, False, lambda d, c: g_text(0, d, c).start())

    @pl.when(k == 1)
    def _():
        @pl.when(h == 0)
        def _():
            @pl.loop(0, CHUNKS)
            def _(i):
                f_relay(i).wait_send()

        image_part(raw.at[B3], ROW_F, N, N, True)

        @pl.when(h == 1)
        def _():
            @pl.loop(0, PIECES)
            def _(p):
                g_far5(p).start()

    far_relay(0)
    far_relay(1)

    @pl.loop(2, 4)
    def _(j):
        pl.when(j == 2)(lambda: slopes(ROW_B + 512, 256, HALF1, 256))
        f_pass(j).wait_send()
        next_part(j, 0, 1024, True)
        g_pass(j).start()

        @pl.when(j == 2)
        def _():
            @pl.loop(3, 8)
            def _(i):
                slopes(ROW_B + i * 256, 256, HALF1, 256)

            share_column()
            far_relay(2)
            next_send(2)
            text_part(second_half, 0, 1024, HALF1, 256, True)
            odd_send(2)
            far_relay(3)

            @pl.when(k == 1)
            def _():
                text_part(second_half, ROW_F, N, HALF1, 256, False)

            text_part(second_half, ROW_O, 1024, HALF1, 256, False, lambda d, c: g_text(1, d, c).start())
            far_relay(4)

    next_send(3)

    @pl.when(k == 0)
    def _():
        image_part(raw.at[M], ROW_M, N, N, False)

    @pl.when(k == 1)
    def _():
        image_part(raw.at[M], ROW_M, N, N, True)

    @pl.loop(0, CHUNKS)
    def _(j):
        g_mate(j).start()

    far_relay(5)

    image_part(own.at[0], ROW_O, N, N, False)
    odd_send(3)
    text_part(own.at[1], ROW_B + 256, 768, 0, N, False)

    share_group()

    def whole(v):
        return jnp.sum(jnp.sum(v, axis=0, keepdims=True), axis=1, keepdims=True)

    def finish(which, r, n, grad):
        r = pl.multiple_of(r, n)
        high, low, q = (uih, uil, pl.ds(pl.multiple_of(ROW_O + r, n), n)) if which == 0 else (uth, utl, pl.ds(r, n))
        u = high[q, :].astype(F32) + low[q, :].astype(F32)
        inv = norms[which, pl.ds(r, n), 0:1]
        along = jnp.sum(u * grad, axis=-1, keepdims=True)
        own[which, pl.ds(r, n), :] = (grad - u * along) * inv

    h1k0 = (h == 1) & (k == 0)

    def store(which, r, n, s):
        dst = (out_img, out_txt)[which]
        r = pl.multiple_of(r, n)
        return pltpu.make_async_copy(own.at[which, pl.ds(r, n)], dst.at[pl.ds(r, n)], ls.at[s])

    @pl.loop(0, PIECES)
    def _(p):
        pl.when(p < 2)(lambda: far_relay(p + 6))
        pl.when(p % 2 == 0)(lambda: g_mate(p // 2).wait_recv())
        g_across(p).wait_recv()

        @pl.when(h1k0)
        def _():
            g_far5(p).wait_recv()
            ret[R3, piece(p), :] += ret[R5, piece(p), :]

        finish(0, p * S, S, own[0, piece(p), :] + ret[R1, piece(p), :] + ret[R3, piece(p), :])
        store(0, p * S, S, p).start()

        @pl.when(p % 4 == 2)
        def _():
            q = p // 4
            columns(lambda d, c: g_text(q, d, c).wait_recv())

            @pl.loop(0, 2)
            def _(i):
                start = pl.multiple_of(q * 256 + i * R, R)
                r = pl.ds(start, R)
                finish(1, start, R, own[1, r, :] + ret[R4, r, :])

            store(1, pl.multiple_of(q * 256, 256), 256, PIECES + q).start()

    for o in range(1, 16):
        share(o).wait_recv()
    final = group[0]
    for o in range(1, 16):
        final = final + group[o]

    count = 65536.0
    sums[0] = whole(final[0:1, :]) / count
    sums[1] = scale11 * whole(final[1:2, :]) / count
    sums[2] = whole(final[2:3, :]) / count
    give_sums = [
        pltpu.make_async_copy(sums.at[q], dst, vs.at[2 + q])
        for q, dst in enumerate((out_loss, out_scale, out_offset))
    ]
    for give in give_sums:
        give.start()

    @pl.loop(0, CHUNKS)
    def _(i):
        f_text(i).wait_send()
        f_mate(i).wait_send()
        pl.when((h == 1) | (k == 1))(lambda: f_across(i).wait_send())
        pl.when(k == 0)(lambda: f_far(i).wait_send())
        g_pass(i).wait_send()
        g_mate(i).wait_send()

    @pl.loop(0, PIECES)
    def _(p):
        g_across(p).wait_send()
        pl.when(k == 1)(lambda: g_far5(p).wait_send())
        store(0, p * S, S, p).wait()

    for q in range(2):
        columns(lambda d, c, q=q: g_text(q, d, c).wait_send())
        store(1, q * 256, 256, PIECES + q).wait()
    for o in range(1, 8):
        column_share(o).wait_send()
    for o in range(1, 16):
        share(o).wait_send()
    for give in give_sums:
        give.wait()


def hand_over(a, b, c, d, e, oa, ob, oc, od, oe, held, held_c, held_d, held_e, sem):
    def steps(src, here, dst, s):
        return pltpu.make_async_copy(src, here, sem.at[0, s]), pltpu.make_async_copy(here, dst, sem.at[1, s])

    order = [steps(c, held_c, oc, 0), steps(d, held_d, od, 1), steps(e, held_e, oe, 2)]
    for i in range(CHUNKS):
        r = pl.ds(i * R, R)
        order.append(steps(a.at[r], held.at[0, r], oa.at[r], 3 + 2 * i))
        order.append(steps(b.at[r], held.at[1, r], ob.at[r], 4 + 2 * i))
    for fetch, _ in order:
        fetch.start()
    for fetch, give in order:
        fetch.wait()
        give.start()
    for _, give in order:
        give.wait()


def shards(picture_vectors, caption_vectors, scale_exponent, offset_shift):
    dma = pltpu.SemaphoreType.DMA
    any_space = pl.BlockSpec(memory_space=pl.ANY)
    block = jax.ShapeDtypeStruct((N, D), F32)
    one = jax.ShapeDtypeStruct((1, 1), F32)
    picture, caption, loss, scale_deriv, offset_deriv = pl.pallas_call(
        kernel,
        out_shape=(block, block, one, one, one),
        in_specs=[any_space] * 4,
        out_specs=(any_space,) * 5,
        scratch_shapes=[
            pltpu.VMEM((ROWS, D), BF16),
            pltpu.VMEM((ROWS, D), BF16),
            pltpu.VMEM((2 * N, D), BF16),
            pltpu.VMEM((2 * N, D), BF16),
            pltpu.VMEM((ROWS, 2 * N), BF16),
            pltpu.VMEM((ROWS, 2 * N), BF16),
            pltpu.VMEM((5, N, D), F32),
            pltpu.VMEM((5, N, D), F32),
            pltpu.VMEM((2, N, D), F32),
            pltpu.VMEM((2, N, 128), F32),
            pltpu.VMEM((24, 128), F32),
            pltpu.VMEM((8, 8, 128), F32),
            pltpu.VMEM((16, 8, 128), F32),
            pltpu.VMEM((2, 1, 1), F32),
            pltpu.VMEM((3, 1, 1), F32),
            dma((6, CHUNKS)),
            dma((5, CHUNKS)),
            dma((4, PIECES)),
            dma((5, PIECES)),
            dma((10,)),
            dma((10,)),
            dma((8,)),
            dma((8,)),
            dma((16,)),
            dma((16,)),
            dma((PIECES + 2,)),
            dma((5,)),
        ],
        name="contrastive_window",
        compiler_params=pltpu.CompilerParams(
            collective_id=0, has_side_effects=True, vmem_limit_bytes=63 * 2**20
        ),
    )(
        scale_exponent.reshape(1, 1),
        offset_shift.reshape(1, 1),
        picture_vectors[0],
        caption_vectors[0],
    )
    picture, caption, loss, scale_deriv, offset_deriv = pl.pallas_call(
        hand_over,
        out_shape=(block, block, one, one, one),
        in_specs=[any_space] * 5,
        out_specs=(any_space,) * 5,
        scratch_shapes=[pltpu.VMEM((2, N, D), F32)] + [pltpu.VMEM((1, 1), F32)] * 3 + [dma((2, 3 + 2 * CHUNKS))],
        name="hand_over",
    )(picture, caption, loss, scale_deriv, offset_deriv)
    return (
        picture[None],
        caption[None],
        loss.reshape(()),
        scale_deriv.reshape(()),
        offset_deriv.reshape(()),
    )


def solution(mesh):
    placed = (P("rep", "blk", None), P("rep", "blk", None), P(), P())
    return jax.shard_map(
        shards,
        mesh=mesh,
        in_specs=placed,
        out_specs=(P("rep", "blk", None), P("rep", "blk", None), P(), P(), P()),
        check_vma=False,
    )
```

```python
import jax
import jax.numpy as jnp
from jax import lax
from jax.experimental import pallas as pl
from jax.experimental.pallas import tpu as pltpu
from jax.sharding import PartitionSpec as P

MESH = pl.DeviceIdType.MESH
F32 = jnp.float32
BF16 = jnp.bfloat16
EPSILON = 1e-06

N = 512
D = 1152
CHUNKS = 4
R = N // CHUNKS
PIECES = 8
S = N // PIECES
TURN = 6

ROW_B, ROW_O, ROW_M, ROW_F = 0, 1024, 1536, 2048
ROWS = 2560
M, B1, B2, B3, C = range(5)
R1, R2, R3, R4, R5 = range(5)
NT = (((1,), (1,)), ((), ()))
NN = (((1,), (0,)), ((), ()))
TN = (((0,), (0,)), ((), ()))


def split(x):
    high = x.astype(BF16)
    return high, (x - high.astype(F32)).astype(BF16)


def dot3(ah, al, bh, bl, dims):
    def one(a, b):
        return lax.dot_general(a, b, dims, preferred_element_type=F32)

    return one(ah, bh) + one(ah, bl) + one(al, bh)


def kernel(
    scale_ref, offset_ref, img, txt,
    out_img, out_txt, out_loss, out_scale, out_offset,
    uih, uil, uth, utl, sh, sl, raw, ret, own, norms, acc, column, group, given, sums,
    fs, fr, bs, br, ts, tr, cs, cr, gs, gr, ls, vs,
):
    blk = lax.axis_index("blk")
    rep = lax.axis_index("rep")
    k = blk % 2
    h = (blk // 2) % 2
    m = blk // 4

    def at(dm, hh, kk):
        return (((m + dm + 16) % 16) * 4 + hh * 2 + kk, rep)

    mate = at(0, h, 1 - k)
    after, before = at(1, h, k), at(-1, h, k)
    across = at(0, 1 - h, k)
    diagonal = at(0, 1 - h, 1 - k)
    far = at(2 * k - 1, h, 1 - k)
    odd = at(2 * h - 1, 1 - h, k)
    level = (m // 4) * 2 + k

    def column_at(o):
        other = (level + o) % 8
        return ((other // 2) * 16 + (m % 4) * 4 + h * 2 + other % 2, rep)

    place = (m % 4) * 4 + h * 2 + rep

    def group_at(o):
        other = (place + o) % 16
        return (m // 4 * 16 + (other // 4) * 4 + ((other // 2) % 2) * 2 + k, other % 2)


    def remote(src, dst, ssem, rsem, dev):
        return pltpu.make_async_remote_copy(
            src_ref=src, dst_ref=dst, send_sem=ssem, recv_sem=rsem, device_id=dev, device_id_type=MESH
        )

    def rows(i):
        return pl.ds(i * R if isinstance(i, int) else pl.multiple_of(i * R, R), R)

    def piece(p):
        return pl.ds(p * S if isinstance(p, int) else pl.multiple_of(p * S, S), S)

    load_img = pltpu.make_async_copy(img, own.at[0], ls.at[0])
    load_txt = pltpu.make_async_copy(txt, own.at[1], ls.at[1])
    load_img.start()
    load_txt.start()
    load_scale = pltpu.make_async_copy(scale_ref, given.at[0], vs.at[0])
    load_offset = pltpu.make_async_copy(offset_ref, given.at[1], vs.at[1])
    load_scale.start()
    load_offset.start()

    barrier = pltpu.get_barrier_semaphore()
    partners = [mate, after, before, across, diagonal, far, odd]
    partners += [column_at(o) for o in range(1, 8)] + [group_at(o) for o in range(1, 16)]
    for dev in partners:
        pl.semaphore_signal(barrier, inc=1, device_id=dev, device_id_type=MESH)
    pl.semaphore_wait(barrier, len(partners))

    def f_text(i):
        return remote(txt.at[rows(i)], raw.at[C, rows(i)], fs.at[0, i], fr.at[C, i], after)

    def f_mate(i):
        return remote(img.at[rows(i)], raw.at[M, rows(i)], fs.at[1, i], fr.at[M, i], mate)

    def f_across(i):
        return remote(img.at[rows(i)], raw.at[B1, rows(i)], fs.at[2, i], fr.at[B1, i], across)

    def f_odd(i):
        return remote(img.at[rows(i)], raw.at[B1, rows(i)], fs.at[2, i], fr.at[B1, i], odd)

    def f_far(i):
        return remote(img.at[rows(i)], raw.at[B3, rows(i)], fs.at[3, i], fr.at[B3, i], far)

    def f_relay(i):
        return remote(raw.at[B3, rows(i)], raw.at[B1, rows(i)], fs.at[4, i], fr.at[B1, i], diagonal)

    def f_pass(i):
        return remote(raw.at[B1, rows(i)], raw.at[B2, rows(i)], fs.at[5, i], fr.at[B2, i], mate)

    h0k1 = (h == 0) & (k == 1)
    h1k1 = (h == 1) & (k == 1)

    @pl.loop(0, CHUNKS)
    def _(i):
        f_text(i).start()
        pl.when(h == 1)(lambda: f_across(i).start())
        pl.when(h0k1 & (i == 0))(lambda: f_odd(i).start())
        pl.when(k == 0)(lambda: f_far(i).start())
        f_mate(i).start()

    load_scale.wait()
    load_offset.wait()
    scale11 = jnp.exp(given[0])
    offset = given[1]
    acc[...] = jnp.zeros_like(acc)

    def unit(x):
        return x * lax.rsqrt(jnp.sum(x * x, axis=-1, keepdims=True) + EPSILON)

    def put_image(slot, i, row):
        high, low = split(unit(raw[slot, rows(i), :]))
        r = pl.ds(pl.multiple_of(row, R), R)
        uih[r, :] = high
        uil[r, :] = low

    def put_text(i):
        high, low = split(unit(raw[C, rows(i), :]))
        r = pl.ds(pl.multiple_of(N + i * R, R), R)
        uth[r, :] = high
        utl[r, :] = low

    def slopes(row, n, col, width, home=None):
        if width == 256:
            return tile(row, n, col, width, home)

        @pl.loop(0, width // 256)
        def _(j):
            tile(row, n, pl.multiple_of(col + j * 256, 256), 256, None if home is None else home - j * 256)

    def tile(row, n, col, width, home):
        r = pl.ds(pl.multiple_of(row, 128), n)
        c = pl.ds(col, width)
        cosine = dot3(uih[r, :], uil[r, :], uth[c, :], utl[c, :], NT)
        z = scale11 * cosine + offset
        if home is not None:
            a = lax.broadcasted_iota(jnp.int32, (n, width), 0) + home
            b = lax.broadcasted_iota(jnp.int32, (n, width), 1)
            sign = jnp.where(a == b, -1.0, 1.0).astype(F32)
            z = sign * z
        e = jnp.exp(z)
        slope = e / (1.0 + e)
        soft = jnp.log1p(e)
        if home is not None:
            slope = sign * slope

        def fold(v):
            v = jnp.sum(v.reshape(n // 8, 8, width), axis=0)
            total = v[:, 0:128]
            for j in range(1, width // 128):
                total = total + v[:, j * 128 : (j + 1) * 128]
            return total

        acc[0:8, :] += fold(soft)
        acc[8:16, :] += fold(slope * cosine)
        acc[16:24, :] += fold(slope)
        high, low = split(scale11 * slope)
        sh[r, c] = high
        sl[r, c] = low

    load_img.wait()
    load_txt.wait()

    @pl.loop(0, CHUNKS)
    def _(i):
        r = pl.ds(pl.multiple_of(i * R, R), R)
        for which in range(2):
            x = own[which, r, :]
            inv = lax.rsqrt(jnp.sum(x * x, axis=-1, keepdims=True) + EPSILON)
            norms[which, r, :] = jnp.broadcast_to(inv, (R, 128))
            high, low = split(x * inv)
            if which == 0:
                q = pl.ds(pl.multiple_of(ROW_O + i * R, R), R)
                uih[q, :] = high
                uil[q, :] = low
            else:
                uth[r, :] = high
                utl[r, :] = low

    @pl.loop(0, 2)
    def _(i):
        slopes(ROW_O + i * 256, 256, 0, 512, home=i * 256)

    @pl.loop(0, CHUNKS)
    def _(i):
        f_mate(i).wait_recv()
        put_image(M, i, ROW_M + i * R)

    def relay(i):
        @pl.when(h0k1)
        def _():
            f_far(i).wait_recv()
            f_relay(i).start()
            pl.when(i + 1 < CHUNKS)(lambda: f_odd(i + 1).start())

    def g_text(q, d, c):
        cut = (pl.ds(q * 256, 256), c)
        return remote(raw.at[(C, *cut)], ret.at[(R4, *cut)], ts.at[q * 3 + d], tr.at[q * 3 + d], before)

    def g_pass(j):
        return remote(raw.at[B2, rows(j)], ret.at[R2, rows(j)], bs.at[0, j], br.at[R2, j], mate)

    def g_mate(j):
        return remote(raw.at[M, rows(j)], ret.at[R1, rows(j)], bs.at[1, j], br.at[R1, j], mate)

    def g_across(p):
        return remote(raw.at[B1, piece(p)], ret.at[R3, piece(p)], bs.at[2, p], br.at[R3, p], across)

    def g_odd(p):
        return remote(raw.at[B1, piece(p)], ret.at[R3, piece(p)], bs.at[2, p], br.at[R3, p], odd)

    def g_ahead(p):
        return remote(raw.at[B1, piece(p)], ret.at[R5, piece(p)], bs.at[2, p], br.at[R5, p], after)

    def g_turn(p):
        return remote(ret.at[R5, piece(p)], ret.at[R3, piece(p)], bs.at[4, p], br.at[R3, p], across)

    def g_relay(p):
        return remote(raw.at[B1, piece(p)], ret.at[R5, piece(p)], bs.at[2, p], br.at[R5, p], diagonal)

    def g_far3(p):
        return remote(raw.at[B3, piece(p)], ret.at[R3, piece(p)], bs.at[3, p], br.at[R3, p], far)

    def g_far5(p):
        return remote(raw.at[B3, piece(p)], ret.at[R5, piece(p)], bs.at[3, p], br.at[R5, p], far)

    def put(dst, value, first):
        if first:
            dst[...] = value
        else:
            dst[...] += value

    def columns(body):
        @pl.loop(0, 2)
        def _(d):
            body(d, pl.ds(pl.multiple_of(d * 512, 512), 512))

        body(2, pl.ds(1024, 128))

    def image_part(dst, row, col, width, first, n=N):
        r, t = pl.ds(row, n), pl.ds(col, width)

        def body(d, c):
            put(dst.at[:, c], dot3(sh[r, t], sl[r, t], uth[t, c], utl[t, c], NN), first)

        columns(body)

    def next_part(j, col, width, first):
        r, t, q = pl.ds(pl.multiple_of(ROW_B + j * 256, 256), 256), pl.ds(col, width), rows(j)

        def body(d, c):
            v = dot3(sh[r, t], sl[r, t], uth[t, c], utl[t, c], NN)
            put(raw.at[B1, q, c], v[0:R, :], first)
            put(raw.at[B2, q, c], v[R:, :], first)

        columns(body)

    def text_part(dst, row, n, col, width, first, then=None):
        r, t = pl.ds(row, n), pl.ds(col, width)

        def body(d, c):
            put(dst.at[:, c], dot3(sh[r, t], sl[r, t], uih[r, c], uil[r, c], TN), first)
            if then is not None:
                then(d, c)

        columns(body)

    first_half, second_half = raw.at[C, pl.ds(0, 256)], raw.at[C, pl.ds(256, 256)]
    HALF0, HALF1 = N, N + 256

    relay(0)

    @pl.when(k == 0)
    def _():
        @pl.loop(0, 2)
        def _(i):
            slopes(ROW_M + i * 256, 256, 0, N)

        image_part(raw.at[M], ROW_M, 0, N, True)

    image_part(own.at[0], ROW_O, 0, N, True)
    relay(1)
    text_part(own.at[1], ROW_O, N, 0, N, True)

    @pl.when(k == 0)
    def _():
        text_part(own.at[1], ROW_M, N, 0, N, False)

    def arrive(i):
        f_across(i).wait_recv()
        f_pass(i).start()
        put_image(B1, i, ROW_B + i * 256)
        pl.when(i < 2)(lambda: relay(i + 2))
        f_text(i).wait_recv()
        put_text(i)
        f_pass(i).wait_recv()
        put_image(B2, i, ROW_B + i * 256 + R)

    @pl.loop(0, 3)
    def _(i):
        arrive(i)

        @pl.when(i < 2)
        def _():
            slopes(ROW_B + i * 256, 256, 0, 512)
            pl.when(i == 0)(lambda: text_part(own.at[1], ROW_B, 256, 0, N, False))

        @pl.when(i == 1)
        def _():
            @pl.loop(0, 6)
            def _(j):
                slopes(jnp.where(j < 2, j * 256, ROW_O + (j - 2) * 256), 256, HALF0, 256)

            text_part(first_half, ROW_B, 512, HALF0, 256, True)
            text_part(first_half, ROW_O, 1024, HALF0, 256, False)
            f_pass(0).wait_send()
            next_part(0, 0, 768, True)

    slopes(ROW_B + 512, 256, 0, 768)
    text_part(first_half, ROW_B + 512, 256, HALF0, 256, False)

    def next_add(j):
        g_pass(j).wait_recv()
        raw[B1, rows(j), :] += ret[R2, rows(j), :]

    def pieces_of(j, body):
        @pl.loop(0, PIECES // CHUNKS)
        def _(e):
            body(j * (PIECES // CHUNKS) + e)

    def relayed_send(j):
        pl.when((h == 1) & (k == 0))(lambda: pieces_of(j, lambda p: g_relay(p).start()))

    def across_send(j):
        pl.when(h == 0)(lambda: pieces_of(j, lambda p: g_across(p).start()))

    def odd_send(j):
        pl.when(h1k1)(lambda: pieces_of(j, odd_piece))

    def odd_piece(p):
        pl.when(p < TURN)(lambda: g_odd(p).start())
        pl.when(p >= TURN)(lambda: g_ahead(p).start())

    def odd_relay(p):
        @pl.when(h1k1)
        def _():
            g_ahead(p).wait_recv()
            g_turn(p).start()

    def next_send(j):
        next_add(j)
        relayed_send(j)
        across_send(j)

    def far_send(first, last):
        @pl.when(h1k1)
        def _():
            @pl.loop(first, last)
            def _(p):
                g_far5(p).start()

    def column_share(o):
        return remote(column.at[level], column.at[level], cs.at[o], cr.at[o], column_at(o))

    def share(o):
        return remote(group.at[place], group.at[place], gs.at[o], gr.at[o], group_at(o))

    def share_column():
        column[level] = jnp.concatenate(
            [jnp.sum(acc[8 * q : 8 * q + 8, :], axis=0, keepdims=True) for q in range(3)]
            + [jnp.zeros((5, 128), F32)],
            axis=0,
        )
        for o in range(1, 8):
            column_share(o).start()

    def share_group():
        for o in range(1, 8):
            column_share(o).wait_recv()
        now = column[0]
        for o in range(1, 8):
            now = now + column[o]
        group[place] = now
        for o in range(1, 16):
            share(o).start()

    def far_relay(p):
        @pl.when(h0k1)
        def _():
            g_relay(p).wait_recv()
            raw[B3, piece(p), :] += ret[R5, piece(p), :]
            g_far3(p).start()

    def first_send():
        text_part(first_half, ROW_B + 768, 256, HALF0, 256, False, lambda d, c: g_text(0, d, c).start())

    def next_full(j):
        f_pass(j).wait_send()
        next_part(j, 0, 1024, True)
        g_pass(j).start()

    f_text(3).wait_recv()
    put_text(3)
    slopes(ROW_B, 256, HALF1, 256)
    next_part(0, HALF1, 256, False)
    g_pass(0).start()
    f_across(3).wait_recv()
    f_pass(3).start()
    put_image(B1, 3, ROW_B + 768)
    slopes(ROW_B + 256, 256, HALF1, 256)
    next_send(0)
    odd_send(0)
    f_pass(3).wait_recv()
    put_image(B2, 3, ROW_B + 768 + R)
    slopes(ROW_B + 768, 256, 0, 768)
    pl.when(k == 0)(first_send)
    next_full(1)
    next_send(1)
    odd_send(1)

    @pl.when(k == 1)
    def _():
        @pl.loop(0, CHUNKS)
        def _(i):
            pl.when(h == 1)(lambda: f_far(i).wait_recv())
            put_image(B3, i, ROW_F + i * R)

        @pl.loop(0, 2)
        def _(i):
            slopes(ROW_F + i * 256, 256, N, N)

        text_part(first_half, ROW_F, N, HALF0, 256, False)
        first_send()

        @pl.when(h == 0)
        def _():
            @pl.loop(0, CHUNKS)
            def _(i):
                f_relay(i).wait_send()

        image_part(raw.at[B3], ROW_F, N, N, True)

    far_send(0, 3)
    for p in range(2):
        far_relay(p)

    slopes(ROW_B + 512, 256, HALF1, 256)
    next_full(2)
    slopes(ROW_B + 768, 256, HALF1, 256)

    @pl.loop(0, 5)
    def _(step):
        def job(on0, on1):
            return pl.when(((k == 0) & (step == on0)) | ((k == 1) & (step == on1)))

        @job(2, 0)
        def _():
            next_send(2)
            odd_send(2)

        @job(3, 1)
        def _():
            next_full(3)
            far_relay(2)

        @job(0, 2)
        def _():
            @pl.loop(0, 4)
            def _(i):
                slopes(ROW_O + i * 256, 256, HALF1, 256)

            share_column()

        @job(4, 3)
        def _():
            next_send(3)
            odd_send(3)
            far_send(3, PIECES)

        @job(1, 4)
        def _():
            far_relay(3)
            text_part(second_half, 0, 1024, HALF1, 256, True)

            @pl.when(k == 1)
            def _():
                text_part(second_half, ROW_F, N, HALF1, 256, False)
            text_part(second_half, ROW_O, 1024, HALF1, 256, False, lambda d, c: g_text(1, d, c).start())

    odd_relay(6)
    odd_relay(7)
    far_relay(4)
    far_relay(5)

    @pl.when(k == 0)
    def _():
        image_part(raw.at[M], ROW_M, N, N, False)

    @pl.when(k == 1)
    def _():
        image_part(raw.at[M], ROW_M, N, N, True)

    @pl.loop(0, CHUNKS)
    def _(j):
        g_mate(j).start()

    image_part(own.at[0], ROW_O, N, N, False)
    far_relay(6)
    share_group()
    text_part(own.at[1], ROW_B + 256, 768, 0, N, False)
    far_relay(7)

    def whole(v):
        return jnp.sum(jnp.sum(v, axis=0, keepdims=True), axis=1, keepdims=True)

    def finish(which, r, n, grad):
        r = pl.multiple_of(r, n)
        high, low, q = (uih, uil, pl.ds(pl.multiple_of(ROW_O + r, n), n)) if which == 0 else (uth, utl, pl.ds(r, n))
        u = high[q, :].astype(F32) + low[q, :].astype(F32)
        inv = norms[which, pl.ds(r, n), 0:1]
        along = jnp.sum(u * grad, axis=-1, keepdims=True)
        own[which, pl.ds(r, n), :] = (grad - u * along) * inv

    h1k0 = (h == 1) & (k == 0)

    def store(which, r, n, s):
        dst = (out_img, out_txt)[which]
        r = pl.multiple_of(r, n)
        return pltpu.make_async_copy(own.at[which, pl.ds(r, n)], dst.at[pl.ds(r, n)], ls.at[s])

    @pl.loop(0, PIECES)
    def _(p):
        pl.when(p % 2 == 0)(lambda: g_mate(p // 2).wait_recv())
        g_across(p).wait_recv()

        @pl.when(h1k0)
        def _():
            g_far5(p).wait_recv()
            ret[R3, piece(p), :] += ret[R5, piece(p), :]

        finish(0, p * S, S, own[0, piece(p), :] + ret[R1, piece(p), :] + ret[R3, piece(p), :])
        store(0, p * S, S, p).start()

        @pl.when(p % 4 == 2)
        def _():
            q = p // 4
            columns(lambda d, c: g_text(q, d, c).wait_recv())

            @pl.loop(0, 2)
            def _(i):
                start = pl.multiple_of(q * 256 + i * R, R)
                r = pl.ds(start, R)
                finish(1, start, R, own[1, r, :] + ret[R4, r, :])

            store(1, pl.multiple_of(q * 256, 256), 256, PIECES + q).start()

    for o in range(1, 16):
        share(o).wait_recv()
    final = group[0]
    for o in range(1, 16):
        final = final + group[o]

    count = 65536.0
    sums[0] = whole(final[0:1, :]) / count
    sums[1] = scale11 * whole(final[1:2, :]) / count
    sums[2] = whole(final[2:3, :]) / count
    give_sums = [
        pltpu.make_async_copy(sums.at[q], dst, vs.at[2 + q])
        for q, dst in enumerate((out_loss, out_scale, out_offset))
    ]
    for give in give_sums:
        give.start()

    @pl.loop(0, CHUNKS)
    def _(i):
        f_text(i).wait_send()
        f_mate(i).wait_send()
        pl.when((h == 1) | (k == 1))(lambda: f_across(i).wait_send())
        pl.when(k == 0)(lambda: f_far(i).wait_send())
        g_pass(i).wait_send()
        g_mate(i).wait_send()

    @pl.loop(0, PIECES)
    def _(p):
        g_across(p).wait_send()
        pl.when(k == 1)(lambda: g_far5(p).wait_send())
        pl.when(h1k1 & (p >= TURN))(lambda: g_turn(p).wait_send())
        store(0, p * S, S, p).wait()

    for q in range(2):
        columns(lambda d, c, q=q: g_text(q, d, c).wait_send())
        store(1, q * 256, 256, PIECES + q).wait()
    for o in range(1, 8):
        column_share(o).wait_send()
    for o in range(1, 16):
        share(o).wait_send()
    for give in give_sums:
        give.wait()


def hand_over(a, b, c, d, e, oa, ob, oc, od, oe, held, held_c, held_d, held_e, sem):
    def steps(src, here, dst, s):
        return pltpu.make_async_copy(src, here, sem.at[0, s]), pltpu.make_async_copy(here, dst, sem.at[1, s])

    order = [steps(c, held_c, oc, 0), steps(d, held_d, od, 1), steps(e, held_e, oe, 2)]
    for i in range(CHUNKS):
        r = pl.ds(i * R, R)
        order.append(steps(a.at[r], held.at[0, r], oa.at[r], 3 + 2 * i))
        order.append(steps(b.at[r], held.at[1, r], ob.at[r], 4 + 2 * i))
    for fetch, _ in order:
        fetch.start()
    for fetch, give in order:
        fetch.wait()
        give.start()
    for _, give in order:
        give.wait()


def shards(picture_vectors, caption_vectors, scale_exponent, offset_shift):
    dma = pltpu.SemaphoreType.DMA
    any_space = pl.BlockSpec(memory_space=pl.ANY)
    block = jax.ShapeDtypeStruct((N, D), F32)
    one = jax.ShapeDtypeStruct((1, 1), F32)
    picture, caption, loss, scale_deriv, offset_deriv = pl.pallas_call(
        kernel,
        out_shape=(block, block, one, one, one),
        in_specs=[any_space] * 4,
        out_specs=(any_space,) * 5,
        scratch_shapes=[
            pltpu.VMEM((ROWS, D), BF16),
            pltpu.VMEM((ROWS, D), BF16),
            pltpu.VMEM((2 * N, D), BF16),
            pltpu.VMEM((2 * N, D), BF16),
            pltpu.VMEM((ROWS, 2 * N), BF16),
            pltpu.VMEM((ROWS, 2 * N), BF16),
            pltpu.VMEM((5, N, D), F32),
            pltpu.VMEM((5, N, D), F32),
            pltpu.VMEM((2, N, D), F32),
            pltpu.VMEM((2, N, 128), F32),
            pltpu.VMEM((24, 128), F32),
            pltpu.VMEM((8, 8, 128), F32),
            pltpu.VMEM((16, 8, 128), F32),
            pltpu.VMEM((2, 1, 1), F32),
            pltpu.VMEM((3, 1, 1), F32),
            dma((6, CHUNKS)),
            dma((5, CHUNKS)),
            dma((5, PIECES)),
            dma((5, PIECES)),
            dma((6,)),
            dma((6,)),
            dma((8,)),
            dma((8,)),
            dma((16,)),
            dma((16,)),
            dma((PIECES + 2,)),
            dma((5,)),
        ],
        name="contrastive_window",
        compiler_params=pltpu.CompilerParams(
            collective_id=0, has_side_effects=True, vmem_limit_bytes=63 * 2**20
        ),
    )(
        scale_exponent.reshape(1, 1),
        offset_shift.reshape(1, 1),
        picture_vectors[0],
        caption_vectors[0],
    )
    picture, caption, loss, scale_deriv, offset_deriv = pl.pallas_call(
        hand_over,
        out_shape=(block, block, one, one, one),
        in_specs=[any_space] * 5,
        out_specs=(any_space,) * 5,
        scratch_shapes=[pltpu.VMEM((2, N, D), F32)] + [pltpu.VMEM((1, 1), F32)] * 3 + [dma((2, 3 + 2 * CHUNKS))],
        name="hand_over",
    )(picture, caption, loss, scale_deriv, offset_deriv)
    return (
        picture[None],
        caption[None],
        loss.reshape(()),
        scale_deriv.reshape(()),
        offset_deriv.reshape(()),
    )


def solution(mesh):
    placed = (P("rep", "blk", None), P("rep", "blk", None), P(), P())
    return jax.shard_map(
        shards,
        mesh=mesh,
        in_specs=placed,
        out_specs=(P("rep", "blk", None), P("rep", "blk", None), P(), P(), P()),
        check_vma=False,
    )
```

```python
import jax
import jax.numpy as jnp
from jax import lax
from jax.experimental import pallas as pl
from jax.experimental.pallas import tpu as pltpu
from jax.sharding import PartitionSpec as P

MESH = pl.DeviceIdType.MESH
F32 = jnp.float32
BF16 = jnp.bfloat16
EPSILON = 1e-06

N = 512
D = 1152
CHUNKS = 4
R = N // CHUNKS
PIECES = 8
S = N // PIECES
TURN = 6

ROW_B, ROW_O, ROW_M, ROW_F = 0, 1024, 1536, 2048
ROWS = 2560
M, B1, B2, B3, C = range(5)
R1, R2, R3, R4, R5 = range(5)
NT = (((1,), (1,)), ((), ()))
NN = (((1,), (0,)), ((), ()))
TN = (((0,), (0,)), ((), ()))


def split(x):
    high = x.astype(BF16)
    return high, (x - high.astype(F32)).astype(BF16)


def dot3(ah, al, bh, bl, dims):
    def one(a, b):
        return lax.dot_general(a, b, dims, preferred_element_type=F32)

    return one(ah, bh) + one(ah, bl) + one(al, bh)


def kernel(
    scale_ref, offset_ref, img, txt,
    out_img, out_txt, out_loss, out_scale, out_offset,
    uih, uil, uth, utl, sh, sl, raw, ret, own, norms, acc, column, group, given, sums,
    fs, fr, bs, br, ts, tr, cs, cr, gs, gr, ls, vs,
):
    blk = lax.axis_index("blk")
    rep = lax.axis_index("rep")
    k = blk % 2
    h = (blk // 2) % 2
    m = blk // 4

    def at(dm, hh, kk):
        return (((m + dm + 16) % 16) * 4 + hh * 2 + kk, rep)

    mate = at(0, h, 1 - k)
    after, before = at(1, h, k), at(-1, h, k)
    across = at(0, 1 - h, k)
    diagonal = at(0, 1 - h, 1 - k)
    far = at(2 * k - 1, h, 1 - k)
    odd = at(2 * h - 1, 1 - h, k)
    level = (m // 4) * 2 + k

    def column_at(o):
        other = (level + o) % 8
        return ((other // 2) * 16 + (m % 4) * 4 + h * 2 + other % 2, rep)

    place = (m % 4) * 4 + h * 2 + rep

    def group_at(o):
        other = (place + o) % 16
        return (m // 4 * 16 + (other // 4) * 4 + ((other // 2) % 2) * 2 + k, other % 2)


    def remote(src, dst, ssem, rsem, dev):
        return pltpu.make_async_remote_copy(
            src_ref=src, dst_ref=dst, send_sem=ssem, recv_sem=rsem, device_id=dev, device_id_type=MESH
        )

    def rows(i):
        return pl.ds(i * R if isinstance(i, int) else pl.multiple_of(i * R, R), R)

    def piece(p):
        return pl.ds(p * S if isinstance(p, int) else pl.multiple_of(p * S, S), S)

    load_img = pltpu.make_async_copy(img, own.at[0], ls.at[0])
    load_txt = pltpu.make_async_copy(txt, own.at[1], ls.at[1])
    load_img.start()
    load_txt.start()
    load_scale = pltpu.make_async_copy(scale_ref, given.at[0], vs.at[0])
    load_offset = pltpu.make_async_copy(offset_ref, given.at[1], vs.at[1])
    load_scale.start()
    load_offset.start()

    barrier = pltpu.get_barrier_semaphore()
    partners = [mate, after, before, across, diagonal, far, odd]
    partners += [column_at(o) for o in range(1, 8)] + [group_at(o) for o in range(1, 16)]
    for dev in partners:
        pl.semaphore_signal(barrier, inc=1, device_id=dev, device_id_type=MESH)
    pl.semaphore_wait(barrier, len(partners))

    def f_text(i):
        return remote(txt.at[rows(i)], raw.at[C, rows(i)], fs.at[0, i], fr.at[C, i], after)

    def f_mate(i):
        return remote(img.at[rows(i)], raw.at[M, rows(i)], fs.at[1, i], fr.at[M, i], mate)

    def f_across(i):
        return remote(img.at[rows(i)], raw.at[B1, rows(i)], fs.at[2, i], fr.at[B1, i], across)

    def f_odd(i):
        return remote(img.at[rows(i)], raw.at[B1, rows(i)], fs.at[2, i], fr.at[B1, i], odd)

    def f_far(i):
        return remote(img.at[rows(i)], raw.at[B3, rows(i)], fs.at[3, i], fr.at[B3, i], far)

    def f_relay(i):
        return remote(raw.at[B3, rows(i)], raw.at[B1, rows(i)], fs.at[4, i], fr.at[B1, i], diagonal)

    def f_pass(i):
        return remote(raw.at[B1, rows(i)], raw.at[B2, rows(i)], fs.at[5, i], fr.at[B2, i], mate)

    h0k1 = (h == 0) & (k == 1)
    h1k1 = (h == 1) & (k == 1)

    @pl.loop(0, CHUNKS)
    def _(i):
        f_text(i).start()
        pl.when(h == 1)(lambda: f_across(i).start())
        pl.when(h0k1 & (i == 0))(lambda: f_odd(i).start())
        pl.when(k == 0)(lambda: f_far(i).start())
        f_mate(i).start()

    load_scale.wait()
    load_offset.wait()
    scale11 = jnp.exp(given[0])
    offset = given[1]
    acc[...] = jnp.zeros_like(acc)

    def unit(x):
        return x * lax.rsqrt(jnp.sum(x * x, axis=-1, keepdims=True) + EPSILON)

    def put_image(slot, i, row):
        high, low = split(unit(raw[slot, rows(i), :]))
        r = pl.ds(pl.multiple_of(row, R), R)
        uih[r, :] = high
        uil[r, :] = low

    def put_text(i):
        high, low = split(unit(raw[C, rows(i), :]))
        r = pl.ds(pl.multiple_of(N + i * R, R), R)
        uth[r, :] = high
        utl[r, :] = low

    def slopes(row, n, col, width, home=None):
        if width == 256:
            return tile(row, n, col, width, home)

        @pl.loop(0, width // 256)
        def _(j):
            tile(row, n, pl.multiple_of(col + j * 256, 256), 256, None if home is None else home - j * 256)

    def tile(row, n, col, width, home):
        r = pl.ds(pl.multiple_of(row, 128), n)
        c = pl.ds(col, width)
        cosine = dot3(uih[r, :], uil[r, :], uth[c, :], utl[c, :], NT)
        z = scale11 * cosine + offset
        if home is not None:
            a = lax.broadcasted_iota(jnp.int32, (n, width), 0) + home
            b = lax.broadcasted_iota(jnp.int32, (n, width), 1)
            sign = jnp.where(a == b, -1.0, 1.0).astype(F32)
            z = sign * z
        e = jnp.exp(z)
        slope = e / (1.0 + e)
        soft = jnp.log1p(e)
        if home is not None:
            slope = sign * slope

        def fold(v):
            v = jnp.sum(v.reshape(n // 8, 8, width), axis=0)
            total = v[:, 0:128]
            for j in range(1, width // 128):
                total = total + v[:, j * 128 : (j + 1) * 128]
            return total

        acc[0:8, :] += fold(soft)
        acc[8:16, :] += fold(slope * cosine)
        acc[16:24, :] += fold(slope)
        high, low = split(scale11 * slope)
        sh[r, c] = high
        sl[r, c] = low

    load_img.wait()
    load_txt.wait()

    @pl.loop(0, CHUNKS)
    def _(i):
        r = pl.ds(pl.multiple_of(i * R, R), R)
        for which in range(2):
            x = own[which, r, :]
            inv = lax.rsqrt(jnp.sum(x * x, axis=-1, keepdims=True) + EPSILON)
            norms[which, r, :] = jnp.broadcast_to(inv, (R, 128))
            high, low = split(x * inv)
            if which == 0:
                q = pl.ds(pl.multiple_of(ROW_O + i * R, R), R)
                uih[q, :] = high
                uil[q, :] = low
            else:
                uth[r, :] = high
                utl[r, :] = low

    @pl.loop(0, 2)
    def _(i):
        slopes(ROW_O + i * 256, 256, 0, 512, home=i * 256)

    @pl.loop(0, CHUNKS)
    def _(i):
        f_mate(i).wait_recv()
        put_image(M, i, ROW_M + i * R)

    def relay(i):
        @pl.when(h0k1)
        def _():
            f_far(i).wait_recv()
            f_relay(i).start()
            pl.when(i + 1 < CHUNKS)(lambda: f_odd(i + 1).start())

    def g_text(q, d, c):
        cut = (pl.ds(q * 256, 256), c)
        return remote(raw.at[(C, *cut)], ret.at[(R4, *cut)], ts.at[q * 3 + d], tr.at[q * 3 + d], before)

    def g_pass(j):
        return remote(raw.at[B2, rows(j)], ret.at[R2, rows(j)], bs.at[0, j], br.at[R2, j], mate)

    def g_mate(j):
        return remote(raw.at[M, rows(j)], ret.at[R1, rows(j)], bs.at[1, j], br.at[R1, j], mate)

    def g_across(p):
        return remote(raw.at[B1, piece(p)], ret.at[R3, piece(p)], bs.at[2, p], br.at[R3, p], across)

    def g_odd(p):
        return remote(raw.at[B1, piece(p)], ret.at[R3, piece(p)], bs.at[2, p], br.at[R3, p], odd)

    def g_ahead(p):
        return remote(raw.at[B1, piece(p)], ret.at[R5, piece(p)], bs.at[2, p], br.at[R5, p], after)

    def g_turn(p):
        return remote(ret.at[R5, piece(p)], ret.at[R3, piece(p)], bs.at[4, p], br.at[R3, p], across)

    def g_relay(p):
        return remote(raw.at[B1, piece(p)], ret.at[R5, piece(p)], bs.at[2, p], br.at[R5, p], diagonal)

    def g_far3(p):
        return remote(raw.at[B3, piece(p)], ret.at[R3, piece(p)], bs.at[3, p], br.at[R3, p], far)

    def g_far5(p):
        return remote(raw.at[B3, piece(p)], ret.at[R5, piece(p)], bs.at[3, p], br.at[R5, p], far)

    def put(dst, value, first):
        if first:
            dst[...] = value
        else:
            dst[...] += value

    def columns(body):
        @pl.loop(0, 2)
        def _(d):
            body(d, pl.ds(pl.multiple_of(d * 512, 512), 512))

        body(2, pl.ds(1024, 128))

    def image_part(dst, row, col, width, first, n=N):
        r, t = pl.ds(row, n), pl.ds(col, width)

        def body(d, c):
            put(dst.at[:, c], dot3(sh[r, t], sl[r, t], uth[t, c], utl[t, c], NN), first)

        columns(body)

    def next_part(j, col, width, first):
        r, t, q = pl.ds(pl.multiple_of(ROW_B + j * 256, 256), 256), pl.ds(col, width), rows(j)

        def body(d, c):
            v = dot3(sh[r, t], sl[r, t], uth[t, c], utl[t, c], NN)
            put(raw.at[B1, q, c], v[0:R, :], first)
            put(raw.at[B2, q, c], v[R:, :], first)

        columns(body)

    def text_part(dst, row, n, col, width, first, then=None):
        r, t = pl.ds(row, n), pl.ds(col, width)

        def body(d, c):
            put(dst.at[:, c], dot3(sh[r, t], sl[r, t], uih[r, c], uil[r, c], TN), first)
            if then is not None:
                then(d, c)

        columns(body)

    first_half, second_half = raw.at[C, pl.ds(0, 256)], raw.at[C, pl.ds(256, 256)]
    HALF0, HALF1 = N, N + 256

    relay(0)

    @pl.when(k == 0)
    def _():
        @pl.loop(0, 2)
        def _(i):
            slopes(ROW_M + i * 256, 256, 0, N)

        image_part(raw.at[M], ROW_M, 0, N, True)

    image_part(own.at[0], ROW_O, 0, N, True)
    relay(1)
    text_part(own.at[1], ROW_O, N, 0, N, True)

    @pl.when(k == 0)
    def _():
        text_part(own.at[1], ROW_M, N, 0, N, False)

    def arrive(i):
        f_across(i).wait_recv()
        f_pass(i).start()
        put_image(B1, i, ROW_B + i * 256)
        pl.when(i < 2)(lambda: relay(i + 2))
        f_text(i).wait_recv()
        put_text(i)
        f_pass(i).wait_recv()
        put_image(B2, i, ROW_B + i * 256 + R)

    @pl.loop(0, 3)
    def _(i):
        arrive(i)

        @pl.when(i < 2)
        def _():
            slopes(ROW_B + i * 256, 256, 0, 512)
            pl.when(i == 0)(lambda: text_part(own.at[1], ROW_B, 256, 0, N, False))

        @pl.when(i == 1)
        def _():
            @pl.loop(0, 6)
            def _(j):
                slopes(jnp.where(j < 2, j * 256, ROW_O + (j - 2) * 256), 256, HALF0, 256)

            text_part(first_half, ROW_B, 512, HALF0, 256, True)
            text_part(first_half, ROW_O, 1024, HALF0, 256, False)
            f_pass(0).wait_send()
            next_part(0, 0, 768, True)

    slopes(ROW_B + 512, 256, 0, 768)
    text_part(first_half, ROW_B + 512, 256, HALF0, 256, False)

    def next_add(j):
        g_pass(j).wait_recv()
        raw[B1, rows(j), :] += ret[R2, rows(j), :]

    def pieces_of(j, body):
        @pl.loop(0, PIECES // CHUNKS)
        def _(e):
            body(j * (PIECES // CHUNKS) + e)

    def relayed_send(j):
        pl.when((h == 1) & (k == 0))(lambda: pieces_of(j, lambda p: g_relay(p).start()))

    def across_send(j):
        pl.when(h == 0)(lambda: pieces_of(j, lambda p: g_across(p).start()))

    def odd_send(j):
        pl.when(h1k1)(lambda: pieces_of(j, odd_piece))

    def odd_piece(p):
        pl.when(p < TURN)(lambda: g_odd(p).start())
        pl.when(p >= TURN)(lambda: g_ahead(p).start())

    def odd_relay(p):
        @pl.when(h1k1)
        def _():
            g_ahead(p).wait_recv()
            g_turn(p).start()

    def next_send(j):
        next_add(j)
        relayed_send(j)
        across_send(j)

    def far_send(first, last):
        @pl.when(h1k1)
        def _():
            @pl.loop(first, last)
            def _(p):
                g_far5(p).start()

    def column_share(o):
        return remote(column.at[level], column.at[level], cs.at[o], cr.at[o], column_at(o))

    def share(o):
        return remote(group.at[place], group.at[place], gs.at[o], gr.at[o], group_at(o))

    def share_column():
        column[level] = jnp.concatenate(
            [jnp.sum(acc[8 * q : 8 * q + 8, :], axis=0, keepdims=True) for q in range(3)]
            + [jnp.zeros((5, 128), F32)],
            axis=0,
        )
        for o in range(1, 8):
            column_share(o).start()

    def share_group():
        for o in range(1, 8):
            column_share(o).wait_recv()
        now = column[0]
        for o in range(1, 8):
            now = now + column[o]
        group[place] = now
        for o in range(1, 16):
            share(o).start()

    def far_relay(p):
        @pl.when(h0k1)
        def _():
            g_relay(p).wait_recv()
            raw[B3, piece(p), :] += ret[R5, piece(p), :]
            g_far3(p).start()

    def first_send():
        text_part(first_half, ROW_B + 768, 256, HALF0, 256, False, lambda d, c: g_text(0, d, c).start())

    def next_full(j):
        f_pass(j).wait_send()
        next_part(j, 0, 1024, True)
        g_pass(j).start()

    f_text(3).wait_recv()
    put_text(3)
    slopes(ROW_B, 256, HALF1, 256)
    next_part(0, HALF1, 256, False)
    g_pass(0).start()
    f_across(3).wait_recv()
    f_pass(3).start()
    put_image(B1, 3, ROW_B + 768)
    slopes(ROW_B + 256, 256, HALF1, 256)
    next_send(0)
    odd_send(0)
    f_pass(3).wait_recv()
    put_image(B2, 3, ROW_B + 768 + R)
    slopes(ROW_B + 768, 256, 0, 768)
    pl.when(k == 0)(first_send)
    next_full(1)
    next_send(1)
    odd_send(1)

    @pl.when(k == 1)
    def _():
        @pl.loop(0, CHUNKS)
        def _(i):
            pl.when(h == 1)(lambda: f_far(i).wait_recv())
            put_image(B3, i, ROW_F + i * R)

        @pl.loop(0, 2)
        def _(i):
            slopes(ROW_F + i * 256, 256, N, N)

        text_part(first_half, ROW_F, N, HALF0, 256, False)
        first_send()

        @pl.when(h == 0)
        def _():
            @pl.loop(0, CHUNKS)
            def _(i):
                f_relay(i).wait_send()

        image_part(raw.at[B3], ROW_F, N, N, True)

    far_send(0, 3)
    for p in range(2):
        far_relay(p)

    slopes(ROW_B + 512, 256, HALF1, 256)
    next_full(2)
    slopes(ROW_B + 768, 256, HALF1, 256)

    @pl.loop(0, 5)
    def _(step):
        def job(on0, on1):
            return pl.when(((k == 0) & (step == on0)) | ((k == 1) & (step == on1)))

        @job(2, 0)
        def _():
            next_send(2)
            odd_send(2)

        @job(3, 1)
        def _():
            next_full(3)
            far_relay(2)

        @job(0, 2)
        def _():
            @pl.loop(0, 4)
            def _(i):
                slopes(ROW_O + i * 256, 256, HALF1, 256)

            share_column()

        @job(4, 3)
        def _():
            next_send(3)
            odd_send(3)
            far_send(3, PIECES)

        @job(1, 4)
        def _():
            far_relay(3)
            text_part(second_half, 0, 1024, HALF1, 256, True)

            @pl.when(k == 1)
            def _():
                text_part(second_half, ROW_F, N, HALF1, 256, False)
            text_part(second_half, ROW_O, 1024, HALF1, 256, False, lambda d, c: g_text(1, d, c).start())

    odd_relay(6)
    odd_relay(7)
    far_relay(4)
    far_relay(5)

    @pl.when(k == 0)
    def _():
        image_part(raw.at[M], ROW_M, N, N, False)

    @pl.when(k == 1)
    def _():
        image_part(raw.at[M], ROW_M, N, N, True)

    @pl.loop(0, CHUNKS)
    def _(j):
        g_mate(j).start()

    image_part(own.at[0], ROW_O, N, N, False)
    far_relay(6)
    share_group()
    text_part(own.at[1], ROW_B + 256, 768, 0, N, False)
    far_relay(7)

    def whole(v):
        return jnp.sum(jnp.sum(v, axis=0, keepdims=True), axis=1, keepdims=True)

    def finish(which, r, n, grad):
        r = pl.multiple_of(r, n)
        high, low, q = (uih, uil, pl.ds(pl.multiple_of(ROW_O + r, n), n)) if which == 0 else (uth, utl, pl.ds(r, n))
        u = high[q, :].astype(F32) + low[q, :].astype(F32)
        inv = norms[which, pl.ds(r, n), 0:1]
        along = jnp.sum(u * grad, axis=-1, keepdims=True)
        own[which, pl.ds(r, n), :] = (grad - u * along) * inv

    h1k0 = (h == 1) & (k == 0)

    def store(which, r, n, s):
        dst = (out_img, out_txt)[which]
        r = pl.multiple_of(r, n)
        return pltpu.make_async_copy(own.at[which, pl.ds(r, n)], dst.at[pl.ds(r, n)], ls.at[s])

    @pl.loop(0, PIECES)
    def _(p):
        pl.when(p % 2 == 0)(lambda: g_mate(p // 2).wait_recv())
        g_across(p).wait_recv()

        @pl.when(h1k0)
        def _():
            g_far5(p).wait_recv()
            ret[R3, piece(p), :] += ret[R5, piece(p), :]

        finish(0, p * S, S, own[0, piece(p), :] + ret[R1, piece(p), :] + ret[R3, piece(p), :])
        store(0, p * S, S, p).start()

        @pl.when(p % 4 == 2)
        def _():
            q = p // 4
            columns(lambda d, c: g_text(q, d, c).wait_recv())

            @pl.loop(0, 2)
            def _(i):
                start = pl.multiple_of(q * 256 + i * R, R)
                r = pl.ds(start, R)
                finish(1, start, R, own[1, r, :] + ret[R4, r, :])

            store(1, pl.multiple_of(q * 256, 256), 256, PIECES + q).start()

    for o in range(1, 16):
        share(o).wait_recv()
    final = group[0]
    for o in range(1, 16):
        final = final + group[o]

    count = 65536.0
    sums[0] = whole(final[0:1, :]) / count
    sums[1] = scale11 * whole(final[1:2, :]) / count
    sums[2] = whole(final[2:3, :]) / count
    give_sums = [
        pltpu.make_async_copy(sums.at[q], dst, vs.at[2 + q])
        for q, dst in enumerate((out_loss, out_scale, out_offset))
    ]
    for give in give_sums:
        give.start()

    @pl.loop(0, CHUNKS)
    def _(i):
        f_text(i).wait_send()
        f_mate(i).wait_send()
        pl.when((h == 1) | (k == 1))(lambda: f_across(i).wait_send())
        pl.when(k == 0)(lambda: f_far(i).wait_send())
        g_pass(i).wait_send()
        g_mate(i).wait_send()

    @pl.loop(0, PIECES)
    def _(p):
        g_across(p).wait_send()
        pl.when(k == 1)(lambda: g_far5(p).wait_send())
        pl.when(h1k1 & (p >= TURN))(lambda: g_turn(p).wait_send())
        store(0, p * S, S, p).wait()

    for q in range(2):
        columns(lambda d, c, q=q: g_text(q, d, c).wait_send())
        store(1, q * 256, 256, PIECES + q).wait()
    for o in range(1, 8):
        column_share(o).wait_send()
    for o in range(1, 16):
        share(o).wait_send()
    for give in give_sums:
        give.wait()


def hand_over(a, b, c, d, e, oa, ob, oc, od, oe, held, held_c, held_d, held_e, sem):
    def steps(src, here, dst, s):
        return pltpu.make_async_copy(src, here, sem.at[0, s]), pltpu.make_async_copy(here, dst, sem.at[1, s])

    order = []
    for i in range(PIECES):
        r = pl.ds(i * S, S)
        order.append(steps(a.at[r], held.at[0, r], oa.at[r], 3 + 2 * i))
        order.append(steps(b.at[r], held.at[1, r], ob.at[r], 4 + 2 * i))
    order += [steps(c, held_c, oc, 0), steps(d, held_d, od, 1), steps(e, held_e, oe, 2)]
    for fetch, _ in order:
        fetch.start()
    for fetch, give in order:
        fetch.wait()
        give.start()
    for _, give in order:
        give.wait()


def shards(picture_vectors, caption_vectors, scale_exponent, offset_shift):
    dma = pltpu.SemaphoreType.DMA
    any_space = pl.BlockSpec(memory_space=pl.ANY)
    block = jax.ShapeDtypeStruct((N, D), F32)
    one = jax.ShapeDtypeStruct((1, 1), F32)
    picture, caption, loss, scale_deriv, offset_deriv = pl.pallas_call(
        kernel,
        out_shape=(block, block, one, one, one),
        in_specs=[any_space] * 4,
        out_specs=(any_space,) * 5,
        scratch_shapes=[
            pltpu.VMEM((ROWS, D), BF16),
            pltpu.VMEM((ROWS, D), BF16),
            pltpu.VMEM((2 * N, D), BF16),
            pltpu.VMEM((2 * N, D), BF16),
            pltpu.VMEM((ROWS, 2 * N), BF16),
            pltpu.VMEM((ROWS, 2 * N), BF16),
            pltpu.VMEM((5, N, D), F32),
            pltpu.VMEM((5, N, D), F32),
            pltpu.VMEM((2, N, D), F32),
            pltpu.VMEM((2, N, 128), F32),
            pltpu.VMEM((24, 128), F32),
            pltpu.VMEM((8, 8, 128), F32),
            pltpu.VMEM((16, 8, 128), F32),
            pltpu.VMEM((2, 1, 1), F32),
            pltpu.VMEM((3, 1, 1), F32),
            dma((6, CHUNKS)),
            dma((5, CHUNKS)),
            dma((5, PIECES)),
            dma((5, PIECES)),
            dma((6,)),
            dma((6,)),
            dma((8,)),
            dma((8,)),
            dma((16,)),
            dma((16,)),
            dma((PIECES + 2,)),
            dma((5,)),
        ],
        name="contrastive_window",
        compiler_params=pltpu.CompilerParams(
            collective_id=0, has_side_effects=True, vmem_limit_bytes=63 * 2**20
        ),
    )(
        scale_exponent.reshape(1, 1),
        offset_shift.reshape(1, 1),
        picture_vectors[0],
        caption_vectors[0],
    )
    picture, caption, loss, scale_deriv, offset_deriv = pl.pallas_call(
        hand_over,
        out_shape=(block, block, one, one, one),
        in_specs=[any_space] * 5,
        out_specs=(any_space,) * 5,
        scratch_shapes=[pltpu.VMEM((2, N, D), F32)] + [pltpu.VMEM((1, 1), F32)] * 3 + [dma((2, 3 + 2 * PIECES))],
        name="hand_over",
    )(picture, caption, loss, scale_deriv, offset_deriv)
    return (
        picture[None],
        caption[None],
        loss.reshape(()),
        scale_deriv.reshape(()),
        offset_deriv.reshape(()),
    )


def solution(mesh):
    placed = (P("rep", "blk", None), P("rep", "blk", None), P(), P())
    return jax.shard_map(
        shards,
        mesh=mesh,
        in_specs=placed,
        out_specs=(P("rep", "blk", None), P("rep", "blk", None), P(), P(), P()),
        check_vma=False,
    )
```
